32 devices in a mesh: dp: 2 (over core), ctx: 16 (over z, y, x).
Axes of the slice: x: 2, y: 2, z: 4, core: 2. Of those that a mesh axis runs over, the one named last changes fastest.
Arguments:
- queries: bfloat16 [8192, 1536], P(('dp', 'ctx')), parts along dimension 0, may hold values from -53 to 53
- keys: bfloat16 [8192, 1536], P(('dp', 'ctx')), parts along dimension 0, may hold values from -6 to 6
- values: bfloat16 [8192, 1536], P(('dp', 'ctx')), parts along dimension 0, may hold values from -6 to 6
- grad_out: bfloat16 [8192, 1536], P(('dp', 'ctx')), parts along dimension 0, may hold values from -6 to 6
- summary_lists: int32 [64, 4], P('dp'), parts along dimension 0, may hold values from 0 to 7, as said below
Outputs:
- attended: bfloat16 [8192, 1536], P(('dp', 'ctx')), parts along dimension 0
- grad_queries: bfloat16 [8192, 1536], P(('dp', 'ctx')), parts along dimension 0
- grad_keys: bfloat16 [8192, 1536], P(('dp', 'ctx')), parts along dimension 0
- grad_values: bfloat16 [8192, 1536], P(('dp', 'ctx')), parts along dimension 0
The draws below stay inside these ranges and needn't reach their ends.
There are 2 independent parts, one for each index of `dp`. The reference program is written for one: setup_inputs(seed, part) draws one part's arguments, and reference() takes and returns one part's arrays. A program takes and returns all parts, laid end to end along the dimension named above; each array names one. Nothing has to cross between parts.
Inputs may be any that keep to these rules, and one draw needn't show every extreme that they name: `summary_lists`: each row names 4 different summary numbers.
All inputs are finite; a program needn't handle non-finite values.
Results may differ from the reference program's by a relative error of at most 0.019.
Values may be sent and summed in bfloat16 or wider, within the bound.
A program may use at most 192 MiB of HBM per device.

```python
import jax
import jax.numpy as jnp
from jax import lax

H = 12
HS = 128
BLK = 128
SUMS = 8
PICKS = 4
TOK_DEV = 256
TOKENS = 4096
NB = 32
STRIDE = 4
N_CTX = 16


def draw_queries(key, part):
    drawn = jax.random.normal(jax.random.fold_in(key, 1), (TOKENS, H * HS), jnp.float32)
    return jnp.clip(drawn, -6.0, 6.0).astype(jnp.bfloat16)


def draw_keys(key, part):
    drawn = jax.random.normal(jax.random.fold_in(key, 2), (TOKENS, H * HS), jnp.float32)
    return jnp.clip(drawn, -6.0, 6.0).astype(jnp.bfloat16)


def draw_summary_lists(key, part):
    row_keys = jax.random.split(jax.random.fold_in(key, 5), NB)

    def one_row(row_key):
        return jax.random.permutation(row_key, SUMS)[:PICKS]
    return jax.vmap(one_row)(row_keys).astype(jnp.int32)


def block_levels(stream_key, extent, pieces, least, high):
    factor_of, own = 1.0, jax.random.fold_in(stream_key, 6)
    for axis_at, parts in pieces:
        draws = jnp.exp(jax.random.uniform(jax.random.fold_in(own, axis_at), (parts,), jnp.float32, least / len(pieces), high / len(pieces)))
        factor_of = factor_of * jnp.repeat(draws, extent[axis_at] // parts).reshape([-1 if axis == axis_at else 1 for axis in range(len(extent))])
    return factor_of


def gaussian(own_key, extent, spread, bound, pieces=(), kind=jnp.bfloat16):
    values = jax.random.normal(own_key, extent, jnp.float32) * spread
    if len(pieces) > 0:
        values = block_levels(own_key, extent, pieces, -0.22, 0.18) * values
    return jnp.clip(values, min=-bound, max=bound).astype(kind)


def setup_inputs(seed: int = 0, part: int = 0) -> dict:
    key_of = jax.random.split(jax.random.key(seed), 6)
    own_keys = jax.random.split(jax.random.fold_in(key_of[5], part), 6)
    queries = draw_queries(jax.random.fold_in(jax.random.fold_in(key_of[5], part), 71), part)
    keys = draw_keys(jax.random.fold_in(jax.random.fold_in(key_of[5], part), 71), part)
    values = gaussian(own_keys[2], (TOKENS, H * HS), 1.0, 6.0, ((0, 16),))
    grad_out = gaussian(own_keys[3], (TOKENS, H * HS), 1.0, 6.0, ((0, 16),))
    summary_lists = draw_summary_lists(jax.random.fold_in(jax.random.fold_in(key_of[5], part), 71), part)
    return dict(queries=queries, keys=keys, values=values, grad_out=grad_out, summary_lists=summary_lists)


def storage_of_doc():
    half_rows = TOK_DEV // 2
    position = jnp.arange(TOKENS, dtype=jnp.int32)
    span_id = position // half_rows
    within = position % half_rows
    owner_dev = jnp.where(span_id < N_CTX, span_id, 2 * N_CTX - 1 - span_id)
    offset = jnp.where(span_id < N_CTX, within, half_rows + within)
    return (owner_dev * TOK_DEV + offset).astype(jnp.int32)


def doc_of_storage():
    half_rows = TOK_DEV // 2
    row_ids = jnp.arange(TOKENS, dtype=jnp.int32)
    owner_dev = row_ids // TOK_DEV
    within = row_ids % TOK_DEV
    first = owner_dev * half_rows + within
    second = (2 * N_CTX - 1 - owner_dev) * half_rows + within - half_rows
    return jnp.where(within < half_rows, first, second).astype(jnp.int32)


def attend_block(query_blk, key_rows, value_rows, grad_blk, visible, scale):
    query_f = query_blk.astype(jnp.float32)
    key_f = key_rows.astype(jnp.float32)
    value_f = value_rows.astype(jnp.float32)
    grad_f = grad_blk.astype(jnp.float32)
    scores = jnp.einsum("gqhd,gkhd->ghqk", query_f, key_f) * scale
    scores = jnp.where(visible[:, None], scores, -1e30)
    highest = jnp.max(scores, axis=-1, keepdims=True)
    weights = jnp.where(visible[:, None], jnp.exp(scores - highest), 0.0)
    probs = weights / jnp.sum(weights, axis=-1, keepdims=True)
    probs_low = probs.astype(jnp.bfloat16)
    attended = jnp.einsum("ghqk,gkhd->gqhd", probs_low.astype(jnp.float32), value_f).astype(jnp.bfloat16)
    delta = jnp.sum(grad_f * attended.astype(jnp.float32), axis=-1)
    dprob = jnp.einsum("gqhd,gkhd->ghqk", grad_f, value_f)
    dscore = (probs * (dprob - jnp.transpose(delta, (0, 2, 1))[..., None])).astype(jnp.bfloat16)
    dscore_f = dscore.astype(jnp.float32)
    grad_query = (jnp.einsum("ghqk,gkhd->gqhd", dscore_f, key_f) * scale).astype(jnp.bfloat16)
    grad_key = jnp.einsum("ghqk,gqhd->gkhd", dscore_f, query_f) * scale
    grad_value = jnp.einsum("ghqk,gqhd->gkhd", probs_low.astype(jnp.float32), grad_f)
    return attended, grad_query, grad_key, grad_value


def reference(queries, keys, values, grad_out, summary_lists):
    feat_width = queries.shape[1]
    scale = HS ** -0.5
    kcount = 2 + PICKS
    gather_rows = storage_of_doc()

    def to_doc(array):
        return jnp.take(array, gather_rows, axis=0).reshape(NB, BLK, H, HS)

    doc_queries = to_doc(queries)
    doc_keys = to_doc(keys)
    doc_values = to_doc(values)
    doc_grads = to_doc(grad_out)
    causal = jnp.arange(BLK)[:, None] >= jnp.arange(BLK)[None, :]
    kinds = jnp.arange(kcount)[:, None, None]

    def step(carry, block_id):
        acc_keys, acc_values = carry
        picks = (summary_lists[block_id] * STRIDE + STRIDE - 1).astype(jnp.int32)
        previous = jnp.maximum(block_id - 1, 0)
        key_ids = jnp.concatenate([previous[None], block_id[None], picks]).astype(jnp.int32)
        live = jnp.concatenate([(block_id >= 1)[None], jnp.ones((1,), bool), picks < block_id - 1])
        visible = jnp.where(kinds == 1, causal[None], live[:, None, None])
        visible = jnp.transpose(visible, (1, 0, 2)).reshape(BLK, kcount * BLK)
        key_rows = doc_keys[key_ids].reshape(kcount * BLK, H, HS)
        value_rows = doc_values[key_ids].reshape(kcount * BLK, H, HS)
        attended, grad_query, grad_key, grad_value = attend_block(
            doc_queries[block_id][None], key_rows[None], value_rows[None], doc_grads[block_id][None], visible[None], scale)
        acc_keys = acc_keys.at[key_ids].add(grad_key.reshape(kcount, BLK, H, HS))
        acc_values = acc_values.at[key_ids].add(grad_value.reshape(kcount, BLK, H, HS))
        return (acc_keys, acc_values), (attended[0], grad_query[0])

    start = (jnp.zeros((NB, BLK, H, HS), jnp.float32), jnp.zeros((NB, BLK, H, HS), jnp.float32))
    (acc_keys, acc_values), (outs, grads_q) = lax.scan(step, start, jnp.arange(NB, dtype=jnp.int32))
    back_rows = doc_of_storage()

    def to_storage(array):
        return jnp.take(array.reshape(TOKENS, feat_width), back_rows, axis=0)

    return (to_storage(outs), to_storage(grads_q),
            to_storage(acc_keys.astype(jnp.bfloat16)), to_storage(acc_values.astype(jnp.bfloat16)))
```

```python
import functools

import jax
import jax.numpy as jnp
from jax import lax
from jax.experimental import pallas as pl
from jax.experimental.pallas import tpu as pltpu
from jax.sharding import PartitionSpec as P

H = 12
HS = 128
BLK = 128
SUMS = 8
PICKS = 4
GRP = 4
HG = H // GRP
WID = HG * HS
HIDDEN = -1e30
MESH = pl.DeviceIdType.MESH


def both(*terms):
    return functools.reduce(jnp.logical_and, terms)


def either(*terms):
    return functools.reduce(jnp.logical_or, terms)


def home(span, groups):
    return jnp.where(span < groups, span, 2 * groups - 1 - span)


def is_summary(span, every):
    return lax.rem(jnp.asarray(span + 1, jnp.int32), jnp.int32(every)) == 0


def needed(span, group, groups, every):
    span = jnp.asarray(span, jnp.int32)
    group = jnp.asarray(group, jnp.int32)
    return both(
        span <= 2 * groups - 2 - group,
        home(span, groups) != group,
        either(is_summary(span, every), span + 1 == group, span + 1 == 2 * groups - 1 - group),
    )


def dot_nt(a, b):
    return lax.dot_general(a, b, (((1,), (1,)), ((), ())), preferred_element_type=jnp.float32)


def dot_tn(a, b):
    return lax.dot_general(a, b, (((0,), (0,)), ((), ())), preferred_element_type=jnp.float32)


def dot_nn(a, b):
    return lax.dot_general(a, b, (((1,), (0,)), ((), ())), preferred_element_type=jnp.float32)


def member_rows(half, k):
    return (k, slice(0, BLK)) if half == 0 else (GRP - 1 - k, slice(BLK, 2 * BLK))


def kernel(
    groups,
    every,
    q_in, k_in, v_in, g_in, bias,
    o_out, dq_out, dk_out, dv_out,
    q_buf, k_buf, v_buf, g_buf, kvs,
    o_buf, dq_buf, dk_buf, dv_buf,
    sacc, gstage, grecv, last_acc, late,
    in_send, in_recv, loc_in, z_send, z_recv, g_send, g_recv, out_send, out_recv, loc_out,
):
    spans = 2 * groups
    slots = spans - 1
    here = lax.axis_index("ctx")
    group = here // GRP
    member = lax.rem(here, GRP)
    scale = HS ** (-0.5)

    barrier = pltpu.get_barrier_semaphore()
    for off in range(1, GRP):
        peer = group * GRP + lax.rem(member + off, GRP)
        pl.semaphore_signal(barrier, inc=1, device_id={"ctx": peer}, device_id_type=MESH)
    for off in range(1, groups):
        peer = lax.rem(group + off, groups) * GRP + member
        pl.semaphore_signal(barrier, inc=1, device_id={"ctx": peer}, device_id_type=MESH)

    ins = (k_in, v_in, q_in, g_in)
    bufs = (k_buf, v_buf, q_buf, g_buf)
    mine = pl.ds(pl.multiple_of(member * WID, WID), WID)
    for a in range(4):
        pltpu.make_async_copy(ins[a].at[:, mine], bufs[a].at[member], loc_in.at[a]).start()
    for s in range(slots):

        @pl.when(both(jnp.logical_not(needed(s, group, groups, every)), group != s))
        def _():
            kvs[s] = jnp.zeros(kvs.shape[1:], kvs.dtype)

    pl.semaphore_wait(barrier, GRP - 1 + groups - 1)

    front = pl.multiple_of(jnp.where(member < 2, BLK, 0), BLK)
    back = pl.multiple_of(BLK - front, BLK)
    plan = ((0, front), (1, front), (0, back), (1, back), (2, None), (3, None))
    for kind, (a, row) in enumerate(plan):
        rows = pl.ds(0, 2 * BLK) if row is None else pl.ds(row, BLK)
        for m in range(GRP):

            @pl.when(member != m)
            def _():
                pltpu.make_async_remote_copy(
                    src_ref=ins[a].at[rows, pl.ds(m * WID, WID)],
                    dst_ref=bufs[a].at[member, rows, :],
                    send_sem=in_send.at[a],
                    recv_sem=in_recv.at[kind, member],
                    device_id={"ctx": group * GRP + m},
                    device_id_type=MESH,
                ).start()

    def arrived(kind):
        a = plan[kind][0]
        for m in range(GRP):
            first = BLK if m < 2 else 0
            if kind < 2:
                rows = pl.ds(first, BLK)
            elif kind < 4:
                rows = pl.ds(BLK - first, BLK)
            else:
                rows = pl.ds(0, 2 * BLK)

            @pl.when(member != m)
            def _():
                ref = bufs[a].at[m, rows, :]
                pltpu.make_async_copy(ref, ref, in_recv.at[kind, m]).wait()

    for a in range(4):
        pltpu.make_async_copy(ins[a].at[:, mine], bufs[a].at[member], loc_in.at[a]).wait()
    arrived(0)
    arrived(1)

    def span_copy(which, kv, p):
        span = group if which == 0 else spans - 1 - group
        m, rows = member_rows(which, GRP - 1)
        slot = jnp.minimum(span, slots - 1)
        return needed(span, p, groups, every), pltpu.make_async_remote_copy(
            src_ref=(k_buf, v_buf)[kv].at[m, rows, :],
            dst_ref=kvs.at[slot, kv],
            send_sem=z_send.at[which, kv, p],
            recv_sem=z_recv.at[slot, kv],
            device_id={"ctx": p * GRP + member},
            device_id_type=MESH,
        )

    for p in range(groups):
        for which in range(2):
            for kv in range(2):
                wanted, copy = span_copy(which, kv, p)

                @pl.when(wanted)
                def _():
                    copy.start()

    kvs[group, 0] = k_buf[GRP - 1, 0:BLK, :]
    kvs[group, 1] = v_buf[GRP - 1, 0:BLK, :]

    for kind in range(2, 6):
        arrived(kind)
    for s in range(slots):

        @pl.when(needed(s, group, groups, every))
        def _():
            for kv in range(2):
                pltpu.make_async_copy(kvs.at[s, kv], kvs.at[s, kv], z_recv.at[s, kv]).wait()

    key_at = lax.broadcasted_iota(jnp.int32, (BLK, BLK), 0)
    query_at = lax.broadcasted_iota(jnp.int32, (BLK, BLK), 1)
    own_bias = jnp.where(key_at <= query_at, 0.0, HIDDEN).astype(jnp.float32)

    def one_span(half, n, h):
        cols = pl.ds(pl.multiple_of(h * HS, HS), HS)
        at = [member_rows(half, k) for k in range(GRP)]
        q = [q_buf[m, r, cols] for m, r in at]
        g = [g_buf[m, r, cols] for m, r in at]
        kb = [k_buf[m, r, cols] for m, r in at]
        vb = [v_buf[m, r, cols] for m, r in at]
        q_all = jnp.concatenate(q, axis=0)
        g_all = jnp.concatenate(g, axis=0)
        k_sum = kvs[0:n, 0, :, cols].reshape(n * BLK, HS)
        v_sum = kvs[0:n, 1, :, cols].reshape(n * BLK, HS)
        k_two = [jnp.concatenate([kb[max(k - 1, 0)], kb[k]], axis=0) for k in range(GRP)]
        v_two = [jnp.concatenate([vb[max(k - 1, 0)], vb[k]], axis=0) for k in range(GRP)]
        lanes = [slice(k * BLK, (k + 1) * BLK) for k in range(GRP)]

        s_sum = dot_nt(k_sum, q_all).reshape(n, BLK, GRP * BLK) * scale
        s_sum = (s_sum + bias[half, 0:n][:, None, :]).reshape(n * BLK, GRP * BLK)
        local = []
        for k in range(GRP):
            before = jnp.full((BLK, BLK), HIDDEN if k == 0 else 0.0, jnp.float32)
            mask = jnp.concatenate([before, own_bias], axis=0)
            local.append(dot_nt(k_two[k], q[k]) * scale + mask)
        s_loc = jnp.concatenate(local, axis=1)
        top = jnp.maximum(
            jnp.max(s_sum, axis=0, keepdims=True), jnp.max(s_loc, axis=0, keepdims=True)
        )
        p_sum = jnp.exp(s_sum - top)
        p_loc = jnp.exp(s_loc - top)
        total = jnp.sum(p_sum, axis=0, keepdims=True) + jnp.sum(p_loc, axis=0, keepdims=True)
        inv = 1.0 / total
        p_sum = p_sum * inv
        p_loc = p_loc * inv
        low_sum = p_sum.astype(jnp.bfloat16)
        low_loc = p_loc.astype(jnp.bfloat16)

        o_t = dot_tn(v_sum, low_sum) + jnp.concatenate(
            [dot_tn(v_two[k], low_loc[:, lanes[k]]) for k in range(GRP)], axis=1
        )
        o_t = o_t.astype(jnp.bfloat16).astype(jnp.float32)
        g_t = jnp.transpose(g_all.astype(jnp.float32))
        delta = jnp.sum(g_t * o_t, axis=0, keepdims=True)
        attended = jnp.transpose(o_t).astype(jnp.bfloat16)

        dp_sum = dot_nt(v_sum, g_all)
        dp_loc = jnp.concatenate([dot_nt(v_two[k], g[k]) for k in range(GRP)], axis=1)
        ds_sum = (p_sum * (dp_sum - delta)).astype(jnp.bfloat16)
        ds_loc = (p_loc * (dp_loc - delta)).astype(jnp.bfloat16)
        dq_t = dot_tn(k_sum, ds_sum) + jnp.concatenate(
            [dot_tn(k_two[k], ds_loc[:, lanes[k]]) for k in range(GRP)], axis=1
        )
        grad_q = (jnp.transpose(dq_t) * scale).astype(jnp.bfloat16)
        for k, (m, r) in enumerate(at):
            o_buf[m, h, r, :] = attended[lanes[k], :]
            dq_buf[m, h, r, :] = grad_q[lanes[k], :]

        dk_sum = (dot_nn(ds_sum, q_all) * scale).reshape(n, BLK, HS)
        dv_sum = dot_nn(low_sum, g_all).reshape(n, BLK, HS)
        dk_two = [dot_nn(ds_loc[:, lanes[k]], q[k]) * scale for k in range(GRP)]
        dv_two = [dot_nn(low_loc[:, lanes[k]], g[k]) for k in range(GRP)]
        for two, buf, kv in ((dk_two, dk_buf, 0), (dv_two, dv_buf, 1)):
            for k, (m, r) in enumerate(at):
                if k < GRP - 1:
                    buf[m, h, r, :] = (two[k][BLK:] + two[k + 1][:BLK]).astype(jnp.bfloat16)
                else:
                    last_acc[half, h, kv] = two[k][BLK:]
        return dk_sum, dv_sum

    outs = (o_out, dq_out, dk_out, dv_out)
    obufs = (o_buf, dq_buf, dk_buf, dv_buf)

    def grad_copy(s, h):
        return pltpu.make_async_remote_copy(
            src_ref=gstage.at[s, h],
            dst_ref=grecv.at[0 if s < groups else 1, group, h],
            send_sem=g_send.at[s, h],
            recv_sem=g_recv.at[0 if s < groups else 1, group, h],
            device_id={"ctx": (s if s < groups else spans - 1 - s) * GRP + member},
            device_id_type=MESH,
        )

    def send_out(a, src, rows, m, h):
        cols = pl.ds(pl.multiple_of((member * HG + h) * HS, HS), HS)

        @pl.when(member != m)
        def _():
            pltpu.make_async_remote_copy(
                src_ref=src,
                dst_ref=outs[a].at[rows, cols],
                send_sem=out_send.at[a],
                recv_sem=out_recv.at[a],
                device_id={"ctx": group * GRP + m},
                device_id_type=MESH,
            ).start()

        @pl.when(member == m)
        def _():
            pltpu.make_async_copy(src, outs[a].at[rows, cols], loc_out.at[a]).start()

    def one_head(h, carry):
        n_low = groups - 1
        dk_sum, dv_sum = one_span(0, n_low, h)
        sacc[0:n_low, 0] = dk_sum
        sacc[0:n_low, 1] = dv_sum
        dk_sum, dv_sum = one_span(1, slots, h)
        sacc[0:n_low, 0] += dk_sum[:n_low]
        sacc[0:n_low, 1] += dv_sum[:n_low]
        sacc[n_low:slots, 0] = dk_sum[n_low:]
        sacc[n_low:slots, 1] = dv_sum[n_low:]
        for s in range(slots):

            @pl.when(needed(s, group, groups, every))
            def _():
                gstage[s, h] = sacc[s].astype(jnp.bfloat16)
                grad_copy(s, h).start()

        last_acc[0, h] += sacc[group]
        for a in range(4):
            for m in range(GRP):
                if a < 2 or m in (1, 2):
                    rows = pl.ds(0, 2 * BLK)
                else:
                    rows = pl.ds(0 if m == 0 else BLK, BLK)
                send_out(a, obufs[a].at[m, h, rows, :], rows, m, h)
        return carry

    lax.fori_loop(0, HG, one_head, 0)

    def finish_head(h, carry):
        for which in range(2):
            span = group if which == 0 else spans - 1 - group
            for p in range(groups):

                @pl.when(needed(span, p, groups, every))
                def _():
                    ref = grecv.at[which, p, h]
                    pltpu.make_async_copy(ref, ref, g_recv.at[which, p, h]).wait()
                    last_acc[which, h] += grecv[which, p, h].astype(jnp.float32)

            late[which, h] = last_acc[which, h].astype(jnp.bfloat16)
            m = GRP - 1 if which == 0 else 0
            rows = pl.ds(which * BLK, BLK)
            for kv in range(2):
                send_out(2 + kv, late.at[which, h, kv], rows, m, h)
        return carry

    lax.fori_loop(0, HG, finish_head, 0)

    for a in range(4):
        away = ins[a].at[:, pl.ds(0, (GRP - 1) * WID)]
        pltpu.make_async_copy(away, away, in_send.at[a]).wait()
    for p in range(groups):
        for which in range(2):
            for kv in range(2):
                wanted, copy = span_copy(which, kv, p)

                @pl.when(wanted)
                def _():
                    copy.wait_send()

    for s in range(slots):

        @pl.when(needed(s, group, groups, every))
        def _():
            for h in range(HG):
                grad_copy(s, h).wait_send()

    for a in range(4):
        own = outs[a].at[:, pl.ds(0, WID)]
        away = outs[a].at[:, pl.ds(0, (GRP - 1) * WID)]
        pltpu.make_async_copy(own, own, loc_out.at[a]).wait()
        pltpu.make_async_copy(away, away, out_send.at[a]).wait()
        pltpu.make_async_copy(away, away, out_recv.at[a]).wait()


def on_device(queries, keys, values, grad_out, summary_lists):
    rows, width = queries.shape
    groups = lax.axis_size("ctx") // GRP
    every = groups * GRP * 2 // SUMS // GRP
    slots = 2 * groups - 1
    group = lax.axis_index("ctx") // GRP

    first = jnp.stack([group, 2 * groups - 1 - group]) * GRP
    blocks = first[:, None] + jnp.arange(GRP, dtype=jnp.int32)
    spans = jnp.arange(slots, dtype=jnp.int32)
    ends = spans * GRP + GRP - 1
    number = jnp.where((spans + 1) % every == 0, (spans + 1) // every - 1, -1)
    picks = summary_lists[blocks]
    picked = jnp.any(picks[:, None, :, :] == number[None, :, None, None], axis=-1)
    now = blocks[:, None, :]
    then = ends[None, :, None]
    seen = (then == now - 1) | (picked & (then < now - 1))
    bias = jnp.repeat(jnp.where(seen, 0.0, HIDDEN).astype(jnp.float32), BLK, axis=-1)

    bf16, f32 = jnp.bfloat16, jnp.float32
    dma = pltpu.SemaphoreType.DMA
    anywhere = pl.BlockSpec(memory_space=pl.ANY)
    return pl.pallas_call(
        functools.partial(kernel, groups, every),
        out_shape=[jax.ShapeDtypeStruct((rows, width), bf16)] * 4,
        in_specs=[anywhere] * 4 + [pl.BlockSpec(memory_space=pltpu.VMEM)],
        out_specs=[anywhere] * 4,
        scratch_shapes=[pltpu.VMEM((GRP, rows, WID), bf16)] * 4
        + [pltpu.VMEM((slots, 2, BLK, WID), bf16)]
        + [pltpu.VMEM((GRP, HG, rows, HS), bf16)] * 4
        + [
            pltpu.VMEM((slots, 2, BLK, HS), f32),
            pltpu.VMEM((slots, HG, 2, BLK, HS), bf16),
            pltpu.VMEM((2, groups, HG, 2, BLK, HS), bf16),
            pltpu.VMEM((2, HG, 2, BLK, HS), f32),
            pltpu.VMEM((2, HG, 2, BLK, HS), bf16),
            dma((4,)),
            dma((6, GRP)),
            dma((4,)),
            dma((2, 2, groups)),
            dma((slots, 2)),
            dma((slots, HG)),
            dma((2, groups, HG)),
            dma((4,)),
            dma((4,)),
            dma((4,)),
        ],
        compiler_params=pltpu.CompilerParams(
            collective_id=0, has_side_effects=True, vmem_limit_bytes=56 * 1024 * 1024
        ),
        cost_estimate=pl.CostEstimate(
            flops=6 * 10**9, bytes_accessed=8 * 10**6, transcendentals=3 * 10**6
        ),
    )(queries, keys, values, grad_out, bias)


def solution(mesh):
    rows = P(("dp", "ctx"), None)
    return jax.shard_map(
        on_device,
        mesh=mesh,
        in_specs=(rows, rows, rows, rows, P("dp", None)),
        out_specs=(rows, rows, rows, rows),
        check_vma=False,
    )
```

```python
import functools

import jax
import jax.numpy as jnp
from jax import lax
from jax.experimental import pallas as pl
from jax.experimental.pallas import tpu as pltpu
from jax.sharding import PartitionSpec as P

H = 12
HS = 128
BLK = 128
SUMS = 8
PICKS = 4
GRP = 4
HG = H // GRP
WID = HG * HS
HIDDEN = -1e30
MESH = pl.DeviceIdType.MESH


def both(*terms):
    return functools.reduce(jnp.logical_and, terms)


def either(*terms):
    return functools.reduce(jnp.logical_or, terms)


def home(span, groups):
    return jnp.where(span < groups, span, 2 * groups - 1 - span)


def is_summary(span, every):
    return lax.rem(jnp.asarray(span + 1, jnp.int32), jnp.int32(every)) == 0


def needed(span, group, groups, every):
    span = jnp.asarray(span, jnp.int32)
    group = jnp.asarray(group, jnp.int32)
    return both(
        span <= 2 * groups - 2 - group,
        home(span, groups) != group,
        either(is_summary(span, every), span + 1 == group, span + 1 == 2 * groups - 1 - group),
    )


def dot_nt(a, b):
    return lax.dot_general(a, b, (((1,), (1,)), ((), ())), preferred_element_type=jnp.float32)


def dot_tn(a, b):
    return lax.dot_general(a, b, (((0,), (0,)), ((), ())), preferred_element_type=jnp.float32)


def dot_nn(a, b):
    return lax.dot_general(a, b, (((1,), (0,)), ((), ())), preferred_element_type=jnp.float32)


def member_rows(half, k):
    return (k, slice(0, BLK)) if half == 0 else (GRP - 1 - k, slice(BLK, 2 * BLK))


def kernel(
    groups,
    every,
    q_in, k_in, v_in, g_in, bias,
    o_out, dq_out, dk_out, dv_out,
    kv_buf, qg_buf, kvs,
    o_buf, dq_buf, dk_buf, dv_buf,
    sacc, gstage, grecv, last_acc, late,
    in_send, first_recv, rest_recv, qg_recv, loc_kv, loc_qg,
    z_send, z_recv, g_send, g_recv, out_send, out_recv, loc_out,
):
    spans = 2 * groups
    slots = spans - 1
    here = lax.axis_index("ctx")
    group = here // GRP
    member = lax.rem(here, GRP)
    scale = HS ** (-0.5)

    barrier = pltpu.get_barrier_semaphore()
    for off in range(1, GRP):
        peer = group * GRP + lax.rem(member + off, GRP)
        pl.semaphore_signal(barrier, inc=1, device_id={"ctx": peer}, device_id_type=MESH)
    for off in range(1, groups):
        peer = lax.rem(group + off, groups) * GRP + member
        pl.semaphore_signal(barrier, inc=1, device_id={"ctx": peer}, device_id_type=MESH)

    def head_cols(m, h):
        return pl.ds(pl.multiple_of((m * HG + h) * HS, HS), HS)

    for h in range(HG):
        cols = head_cols(member, h)
        for half in range(2):
            rows = pl.ds(half * BLK, BLK)
            for kv, ref in enumerate((k_in, v_in)):
                pltpu.make_async_copy(
                    ref.at[rows, cols], kv_buf.at[member, h, half, kv], loc_kv.at[h]
                ).start()
        for i, ref in enumerate((q_in, g_in)):
            pltpu.make_async_copy(ref.at[:, cols], qg_buf.at[member, h, i], loc_qg.at[h]).start()
    for s in range(slots):

        @pl.when(both(jnp.logical_not(needed(s, group, groups, every)), group != s))
        def _():
            kvs[s] = jnp.zeros(kvs.shape[1:], kvs.dtype)

    pl.semaphore_wait(barrier, GRP - 1 + groups - 1)

    front = jnp.where(member < 2, 1, 0)

    def send_kv(h, half, recv):
        rows = pl.ds(pl.multiple_of(half * BLK, BLK), BLK)
        for m in range(GRP):

            @pl.when(member != m)
            def _():
                for kv, ref in enumerate((k_in, v_in)):
                    pltpu.make_async_remote_copy(
                        src_ref=ref.at[rows, head_cols(m, h)],
                        dst_ref=kv_buf.at[member, h, half, kv],
                        send_sem=in_send.at[kv],
                        recv_sem=recv.at[h, member],
                        device_id={"ctx": group * GRP + m},
                        device_id_type=MESH,
                    ).start()

    def send_qg(h):
        for m in range(GRP):

            @pl.when(member != m)
            def _():
                for i, ref in enumerate((q_in, g_in)):
                    pltpu.make_async_remote_copy(
                        src_ref=ref.at[:, head_cols(m, h)],
                        dst_ref=qg_buf.at[member, h, i],
                        send_sem=in_send.at[2 + i],
                        recv_sem=qg_recv.at[h, member],
                        device_id={"ctx": group * GRP + m},
                        device_id_type=MESH,
                    ).start()

    send_kv(0, front, first_recv)
    send_kv(1, front, first_recv)
    send_kv(0, 1 - front, rest_recv)
    send_qg(0)
    for h in range(1, HG):
        if h + 1 < HG:
            send_kv(h + 1, front, first_recv)
        send_kv(h, 1 - front, rest_recv)
        send_qg(h)

    def span_copy(which, p, h):
        span = group if which == 0 else spans - 1 - group
        m = GRP - 1 if which == 0 else 0
        slot = jnp.minimum(span, slots - 1)
        return needed(span, p, groups, every), pltpu.make_async_remote_copy(
            src_ref=kv_buf.at[m, h, which],
            dst_ref=kvs.at[slot, h],
            send_sem=z_send.at[which, p, h],
            recv_sem=z_recv.at[slot, h],
            device_id={"ctx": p * GRP + member},
            device_id_type=MESH,
        )

    def spread(h):
        mine = kv_buf.at[member, h]
        pltpu.make_async_copy(mine, mine, loc_kv.at[h]).wait()
        for m in range(GRP):

            @pl.when(member != m)
            def _():
                ref = kv_buf.at[m, h, 1 if m < 2 else 0]
                pltpu.make_async_copy(ref, ref, first_recv.at[h, m]).wait()

        for p in range(groups):
            for which in range(2):
                wanted, copy = span_copy(which, p, h)

                @pl.when(wanted)
                def _():
                    copy.start()

        kvs[group, h] = kv_buf[GRP - 1, h, 0]

    def gather(h):
        mine = qg_buf.at[member, h]
        pltpu.make_async_copy(mine, mine, loc_qg.at[h]).wait()
        for m in range(GRP):

            @pl.when(member != m)
            def _():
                ref = kv_buf.at[m, h, 0 if m < 2 else 1]
                pltpu.make_async_copy(ref, ref, rest_recv.at[h, m]).wait()
                ref = qg_buf.at[m, h]
                pltpu.make_async_copy(ref, ref, qg_recv.at[h, m]).wait()

        for s in range(slots):

            @pl.when(needed(s, group, groups, every))
            def _():
                pltpu.make_async_copy(kvs.at[s, h], kvs.at[s, h], z_recv.at[s, h]).wait()

    spread(0)
    spread(1)

    key_at = lax.broadcasted_iota(jnp.int32, (BLK, BLK), 0)
    query_at = lax.broadcasted_iota(jnp.int32, (BLK, BLK), 1)
    own_bias = jnp.where(key_at <= query_at, 0.0, HIDDEN).astype(jnp.float32)

    def one_span(half, n, h):
        at = [member_rows(half, k) for k in range(GRP)]
        q = [qg_buf[m, h, 0, r, :] for m, r in at]
        g = [qg_buf[m, h, 1, r, :] for m, r in at]
        kb = [kv_buf[m, h, half, 0] for m, r in at]
        vb = [kv_buf[m, h, half, 1] for m, r in at]
        q_all = jnp.concatenate(q, axis=0)
        g_all = jnp.concatenate(g, axis=0)
        k_sum = kvs[0:n, h, 0].reshape(n * BLK, HS)
        v_sum = kvs[0:n, h, 1].reshape(n * BLK, HS)
        k_two = [jnp.concatenate([kb[max(k - 1, 0)], kb[k]], axis=0) for k in range(GRP)]
        v_two = [jnp.concatenate([vb[max(k - 1, 0)], vb[k]], axis=0) for k in range(GRP)]
        lanes = [slice(k * BLK, (k + 1) * BLK) for k in range(GRP)]

        s_sum = dot_nt(k_sum, q_all).reshape(n, BLK, GRP * BLK) * scale
        s_sum = (s_sum + bias[half, 0:n][:, None, :]).reshape(n * BLK, GRP * BLK)
        local = []
        for k in range(GRP):
            before = jnp.full((BLK, BLK), HIDDEN if k == 0 else 0.0, jnp.float32)
            mask = jnp.concatenate([before, own_bias], axis=0)
            local.append(dot_nt(k_two[k], q[k]) * scale + mask)
        s_loc = jnp.concatenate(local, axis=1)
        top = jnp.maximum(
            jnp.max(s_sum, axis=0, keepdims=True), jnp.max(s_loc, axis=0, keepdims=True)
        )
        p_sum = jnp.exp(s_sum - top)
        p_loc = jnp.exp(s_loc - top)
        total = jnp.sum(p_sum, axis=0, keepdims=True) + jnp.sum(p_loc, axis=0, keepdims=True)
        inv = 1.0 / total
        p_sum = p_sum * inv
        p_loc = p_loc * inv
        low_sum = p_sum.astype(jnp.bfloat16)
        low_loc = p_loc.astype(jnp.bfloat16)

        o_t = dot_tn(v_sum, low_sum) + jnp.concatenate(
            [dot_tn(v_two[k], low_loc[:, lanes[k]]) for k in range(GRP)], axis=1
        )
        o_t = o_t.astype(jnp.bfloat16).astype(jnp.float32)
        g_t = jnp.transpose(g_all.astype(jnp.float32))
        delta = jnp.sum(g_t * o_t, axis=0, keepdims=True)
        attended = jnp.transpose(o_t).astype(jnp.bfloat16)

        dp_sum = dot_nt(v_sum, g_all)
        dp_loc = jnp.concatenate([dot_nt(v_two[k], g[k]) for k in range(GRP)], axis=1)
        ds_sum = (p_sum * (dp_sum - delta)).astype(jnp.bfloat16)
        ds_loc = (p_loc * (dp_loc - delta)).astype(jnp.bfloat16)
        dq_t = dot_tn(k_sum, ds_sum) + jnp.concatenate(
            [dot_tn(k_two[k], ds_loc[:, lanes[k]]) for k in range(GRP)], axis=1
        )
        grad_q = (jnp.transpose(dq_t) * scale).astype(jnp.bfloat16)
        for k, (m, r) in enumerate(at):
            o_buf[m, h, r, :] = attended[lanes[k], :]
            dq_buf[m, h, r, :] = grad_q[lanes[k], :]

        dk_sum = (dot_nn(ds_sum, q_all) * scale).reshape(n, BLK, HS)
        dv_sum = dot_nn(low_sum, g_all).reshape(n, BLK, HS)
        dk_two = [dot_nn(ds_loc[:, lanes[k]], q[k]) * scale for k in range(GRP)]
        dv_two = [dot_nn(low_loc[:, lanes[k]], g[k]) for k in range(GRP)]
        for two, buf, kv in ((dk_two, dk_buf, 0), (dv_two, dv_buf, 1)):
            for k, (m, r) in enumerate(at):
                if k < GRP - 1:
                    buf[m, h, r, :] = (two[k][BLK:] + two[k + 1][:BLK]).astype(jnp.bfloat16)
                else:
                    last_acc[half, h, kv] = two[k][BLK:]
        return dk_sum, dv_sum

    outs = (o_out, dq_out, dk_out, dv_out)
    obufs = (o_buf, dq_buf, dk_buf, dv_buf)

    def grad_copy(s, h):
        return pltpu.make_async_remote_copy(
            src_ref=gstage.at[s, h],
            dst_ref=grecv.at[0 if s < groups else 1, group, h],
            send_sem=g_send.at[s, h],
            recv_sem=g_recv.at[0 if s < groups else 1, group, h],
            device_id={"ctx": (s if s < groups else spans - 1 - s) * GRP + member},
            device_id_type=MESH,
        )

    def send_out(a, src, rows, m, h):
        cols = pl.ds(pl.multiple_of((member * HG + h) * HS, HS), HS)

        @pl.when(member != m)
        def _():
            pltpu.make_async_remote_copy(
                src_ref=src,
                dst_ref=outs[a].at[rows, cols],
                send_sem=out_send.at[a],
                recv_sem=out_recv.at[a],
                device_id={"ctx": group * GRP + m},
                device_id_type=MESH,
            ).start()

        @pl.when(member == m)
        def _():
            pltpu.make_async_copy(src, outs[a].at[rows, cols], loc_out.at[a]).start()

    def finish_head(h):
        for which in range(2):
            span = group if which == 0 else spans - 1 - group
            for p in range(groups):

                @pl.when(needed(span, p, groups, every))
                def _():
                    ref = grecv.at[which, p, h]
                    pltpu.make_async_copy(ref, ref, g_recv.at[which, p, h]).wait()
                    last_acc[which, h] += grecv[which, p, h].astype(jnp.float32)

            late[which, h] = last_acc[which, h].astype(jnp.bfloat16)
            m = GRP - 1 if which == 0 else 0
            rows = pl.ds(which * BLK, BLK)
            for kv in range(2):
                send_out(2 + kv, late.at[which, h, kv], rows, m, h)

    def one_head(h, carry):
        n_low = groups - 1
        gather(h)
        dk_sum, dv_sum = one_span(0, n_low, h)
        sacc[0:n_low, 0] = dk_sum
        sacc[0:n_low, 1] = dv_sum
        dk_sum, dv_sum = one_span(1, slots, h)
        sacc[0:n_low, 0] += dk_sum[:n_low]
        sacc[0:n_low, 1] += dv_sum[:n_low]
        sacc[n_low:slots, 0] = dk_sum[n_low:]
        sacc[n_low:slots, 1] = dv_sum[n_low:]
        for s in range(slots):

            @pl.when(needed(s, group, groups, every))
            def _():
                gstage[s, h] = sacc[s].astype(jnp.bfloat16)
                grad_copy(s, h).start()

        last_acc[0, h] += sacc[group]
        for a in range(4):
            for m in range(GRP):
                if a < 2 or m in (1, 2):
                    rows = pl.ds(0, 2 * BLK)
                else:
                    rows = pl.ds(0 if m == 0 else BLK, BLK)
                send_out(a, obufs[a].at[m, h, rows, :], rows, m, h)

        @pl.when(h + 2 < HG)
        def _():
            spread(h + 2)

        @pl.when(h > 0)
        def _():
            finish_head(h - 1)

        return carry

    lax.fori_loop(0, HG, one_head, 0)

    finish_head(HG - 1)

    for a in range(4):
        away = (k_in, v_in, q_in, g_in)[a].at[:, pl.ds(0, (GRP - 1) * WID)]
        pltpu.make_async_copy(away, away, in_send.at[a]).wait()
    for p in range(groups):
        for which in range(2):
            for h in range(HG):
                wanted, copy = span_copy(which, p, h)

                @pl.when(wanted)
                def _():
                    copy.wait_send()

    for s in range(slots):

        @pl.when(needed(s, group, groups, every))
        def _():
            for h in range(HG):
                grad_copy(s, h).wait_send()

    for a in range(4):
        own = outs[a].at[:, pl.ds(0, WID)]
        away = outs[a].at[:, pl.ds(0, (GRP - 1) * WID)]
        pltpu.make_async_copy(own, own, loc_out.at[a]).wait()
        pltpu.make_async_copy(away, away, out_send.at[a]).wait()
        pltpu.make_async_copy(away, away, out_recv.at[a]).wait()


def on_device(queries, keys, values, grad_out, summary_lists):
    rows, width = queries.shape
    groups = lax.axis_size("ctx") // GRP
    every = groups * GRP * 2 // SUMS // GRP
    slots = 2 * groups - 1
    group = lax.axis_index("ctx") // GRP

    first = jnp.stack([group, 2 * groups - 1 - group]) * GRP
    blocks = first[:, None] + jnp.arange(GRP, dtype=jnp.int32)
    spans = jnp.arange(slots, dtype=jnp.int32)
    ends = spans * GRP + GRP - 1
    number = jnp.where((spans + 1) % every == 0, (spans + 1) // every - 1, -1)
    picks = summary_lists[blocks]
    picked = jnp.any(picks[:, None, :, :] == number[None, :, None, None], axis=-1)
    now = blocks[:, None, :]
    then = ends[None, :, None]
    seen = (then == now - 1) | (picked & (then < now - 1))
    bias = jnp.repeat(jnp.where(seen, 0.0, HIDDEN).astype(jnp.float32), BLK, axis=-1)

    bf16, f32 = jnp.bfloat16, jnp.float32
    dma = pltpu.SemaphoreType.DMA
    anywhere = pl.BlockSpec(memory_space=pl.ANY)
    return pl.pallas_call(
        functools.partial(kernel, groups, every),
        out_shape=[jax.ShapeDtypeStruct((rows, width), bf16)] * 4,
        in_specs=[anywhere] * 4 + [pl.BlockSpec(memory_space=pltpu.VMEM)],
        out_specs=[anywhere] * 4,
        scratch_shapes=[
            pltpu.VMEM((GRP, HG, 2, 2, BLK, HS), bf16),
            pltpu.VMEM((GRP, HG, 2, rows, HS), bf16),
            pltpu.VMEM((slots, HG, 2, BLK, HS), bf16),
        ]
        + [pltpu.VMEM((GRP, HG, rows, HS), bf16)] * 4
        + [
            pltpu.VMEM((slots, 2, BLK, HS), f32),
            pltpu.VMEM((slots, HG, 2, BLK, HS), bf16),
            pltpu.VMEM((2, groups, HG, 2, BLK, HS), bf16),
            pltpu.VMEM((2, HG, 2, BLK, HS), f32),
            pltpu.VMEM((2, HG, 2, BLK, HS), bf16),
            dma((4,)),
            dma((HG, GRP)),
            dma((HG, GRP)),
            dma((HG, GRP)),
            dma((HG,)),
            dma((HG,)),
            dma((2, groups, HG)),
            dma((slots, HG)),
            dma((slots, HG)),
            dma((2, groups, HG)),
            dma((4,)),
            dma((4,)),
            dma((4,)),
        ],
        compiler_params=pltpu.CompilerParams(
            collective_id=0, has_side_effects=True, vmem_limit_bytes=56 * 1024 * 1024
        ),
        cost_estimate=pl.CostEstimate(
            flops=6 * 10**9, bytes_accessed=8 * 10**6, transcendentals=3 * 10**6
        ),
    )(queries, keys, values, grad_out, bias)


def solution(mesh):
    rows = P(("dp", "ctx"), None)
    return jax.shard_map(
        on_device,
        mesh=mesh,
        in_specs=(rows, rows, rows, rows, P("dp", None)),
        out_specs=(rows, rows, rows, rows),
        check_vma=False,
    )
```

```python
import functools

import jax
import jax.numpy as jnp
from jax import lax
from jax.experimental import pallas as pl
from jax.experimental.pallas import tpu as pltpu
from jax.sharding import PartitionSpec as P

H = 12
HS = 128
BLK = 128
SUMS = 8
PICKS = 4
PIECES = 4
GRP = 4
HG = H // GRP
WID = HG * HS
HIDDEN = -1e30
LOG2_E = 1.4426950408889634
MESH = pl.DeviceIdType.MESH


def both(*terms):
    return functools.reduce(jnp.logical_and, terms)


def either(*terms):
    return functools.reduce(jnp.logical_or, terms)


def home(span, groups):
    return jnp.where(span < groups, span, 2 * groups - 1 - span)


def is_summary(span, every):
    return lax.rem(jnp.asarray(span + 1, jnp.int32), jnp.int32(every)) == 0


def needed(span, group, groups, every):
    span = jnp.asarray(span, jnp.int32)
    group = jnp.asarray(group, jnp.int32)
    return both(
        span <= 2 * groups - 2 - group,
        home(span, groups) != group,
        either(is_summary(span, every), span + 1 == group, span + 1 == 2 * groups - 1 - group),
    )


def dot_nt(a, b):
    return lax.dot_general(a, b, (((1,), (1,)), ((), ())), preferred_element_type=jnp.float32)


def dot_tn(a, b):
    return lax.dot_general(a, b, (((0,), (0,)), ((), ())), preferred_element_type=jnp.float32)


def dot_nn(a, b):
    return lax.dot_general(a, b, (((1,), (0,)), ((), ())), preferred_element_type=jnp.float32)


def member_rows(half, k):
    return (k, slice(0, BLK)) if half == 0 else (GRP - 1 - k, slice(BLK, 2 * BLK))


def kernel(
    groups,
    every,
    q_in, k_in, v_in, g_in, lists,
    o_out, dq_out, dk_out, dv_out,
    kv_buf, qg_buf, kvs,
    o_buf, dq_buf, dk_buf, dv_buf,
    sacc, gstage, grecv, last_acc, late,
    bias, in_send, first_recv, rest_recv, qg_recv, loc_kv, loc_qg,
    z_send, z_recv, g_send, g_recv, out_send, out_recv, loc_out,
):
    spans = 2 * groups
    slots = spans - 1
    here = lax.axis_index("ctx")
    group = here // GRP
    member = lax.rem(here, GRP)
    scale = HS ** (-0.5)
    scale_2 = scale * LOG2_E

    barrier = pltpu.get_barrier_semaphore()
    for off in range(1, GRP):
        peer = group * GRP + lax.rem(member + off, GRP)
        pl.semaphore_signal(barrier, inc=1, device_id={"ctx": peer}, device_id_type=MESH)
    for off in range(1, groups):
        peer = lax.rem(group + off, groups) * GRP + member
        pl.semaphore_signal(barrier, inc=1, device_id={"ctx": peer}, device_id_type=MESH)

    def head_cols(m, h):
        return pl.ds(pl.multiple_of((m * HG + h) * HS, HS), HS)

    for h in range(HG):
        cols = head_cols(member, h)
        for half in range(2):
            rows = pl.ds(half * BLK, BLK)
            for kv, ref in enumerate((k_in, v_in)):
                pltpu.make_async_copy(
                    ref.at[rows, cols], kv_buf.at[member, h, half, kv], loc_kv.at[h]
                ).start()
        for i, ref in enumerate((q_in, g_in)):
            pltpu.make_async_copy(ref.at[:, cols], qg_buf.at[member, h, i], loc_qg.at[h]).start()
    for s in range(slots):

        @pl.when(both(jnp.logical_not(needed(s, group, groups, every)), group != s))
        def _():
            kvs[s] = jnp.zeros(kvs.shape[1:], kvs.dtype)

    pl.semaphore_wait(barrier, GRP - 1 + groups - 1)

    front = jnp.where(member < 2, 1, 0)

    def send_kv(h, half, recv):
        rows = pl.ds(pl.multiple_of(half * BLK, BLK), BLK)
        for m in range(GRP):

            @pl.when(member != m)
            def _():
                for kv, ref in enumerate((k_in, v_in)):
                    pltpu.make_async_remote_copy(
                        src_ref=ref.at[rows, head_cols(m, h)],
                        dst_ref=kv_buf.at[member, h, half, kv],
                        send_sem=in_send.at[kv],
                        recv_sem=recv.at[h, member],
                        device_id={"ctx": group * GRP + m},
                        device_id_type=MESH,
                    ).start()

    def send_qg(h):
        for m in range(GRP):

            @pl.when(member != m)
            def _():
                for i, ref in enumerate((q_in, g_in)):
                    pltpu.make_async_remote_copy(
                        src_ref=ref.at[:, head_cols(m, h)],
                        dst_ref=qg_buf.at[member, h, i],
                        send_sem=in_send.at[2 + i],
                        recv_sem=qg_recv.at[h, member],
                        device_id={"ctx": group * GRP + m},
                        device_id_type=MESH,
                    ).start()

    send_kv(0, front, first_recv)
    send_kv(1, front, first_recv)
    send_kv(0, 1 - front, rest_recv)
    send_qg(0)
    for h in range(1, HG):
        if h + 1 < HG:
            send_kv(h + 1, front, first_recv)
        send_kv(h, 1 - front, rest_recv)
        send_qg(h)

    def span_copy(which, p, h):
        span = group if which == 0 else spans - 1 - group
        m = GRP - 1 if which == 0 else 0
        slot = jnp.minimum(span, slots - 1)
        return needed(span, p, groups, every), pltpu.make_async_remote_copy(
            src_ref=kv_buf.at[m, h, which],
            dst_ref=kvs.at[slot, h],
            send_sem=z_send.at[which, p, h],
            recv_sem=z_recv.at[slot, h],
            device_id={"ctx": p * GRP + member},
            device_id_type=MESH,
        )

    def spread(h):
        mine = kv_buf.at[member, h]
        pltpu.make_async_copy(mine, mine, loc_kv.at[h]).wait()
        for m in range(GRP):

            @pl.when(member != m)
            def _():
                ref = kv_buf.at[m, h, 1 if m < 2 else 0]
                pltpu.make_async_copy(ref, ref, first_recv.at[h, m]).wait()

        for p in range(groups):
            for which in range(2):
                wanted, copy = span_copy(which, p, h)

                @pl.when(wanted)
                def _():
                    copy.start()

        kvs[group, h] = kv_buf[GRP - 1, h, 0]

    def gather(h):
        mine = qg_buf.at[member, h]
        pltpu.make_async_copy(mine, mine, loc_qg.at[h]).wait()
        for m in range(GRP):

            @pl.when(member != m)
            def _():
                ref = kv_buf.at[m, h, 0 if m < 2 else 1]
                pltpu.make_async_copy(ref, ref, rest_recv.at[h, m]).wait()
                ref = qg_buf.at[m, h]
                pltpu.make_async_copy(ref, ref, qg_recv.at[h, m]).wait()

        for s in range(slots):

            @pl.when(needed(s, group, groups, every))
            def _():
                pltpu.make_async_copy(kvs.at[s, h], kvs.at[s, h], z_recv.at[s, h]).wait()

    for half in range(2):
        for k in range(GRP):
            block = (group if half == 0 else spans - 1 - group) * GRP + k
            picks = [lists[block, i] for i in range(PICKS)]
            for s in range(slots):
                end = s * GRP + GRP - 1
                seen = end == block - 1
                if (s + 1) % every == 0:
                    picked = either(*[pick == (s + 1) // every - 1 for pick in picks])
                    seen = either(seen, both(picked, end < block - 1))
                row = jnp.full((1, BLK), jnp.where(seen, 0.0, HIDDEN), jnp.float32)
                bias[half, s, :, k * BLK : (k + 1) * BLK] = row

    spread(0)
    spread(1)

    key_at = lax.broadcasted_iota(jnp.int32, (BLK, BLK), 0)
    query_at = lax.broadcasted_iota(jnp.int32, (BLK, BLK), 1)
    own_bias = jnp.where(key_at <= query_at, 0.0, HIDDEN).astype(jnp.float32)

    def one_span(half, n, h):
        at = [member_rows(half, k) for k in range(GRP)]
        q = [qg_buf[m, h, 0, r, :] for m, r in at]
        g = [qg_buf[m, h, 1, r, :] for m, r in at]
        kb = [kv_buf[m, h, half, 0] for m, r in at]
        vb = [kv_buf[m, h, half, 1] for m, r in at]
        q_all = jnp.concatenate(q, axis=0)
        g_all = jnp.concatenate(g, axis=0)
        k_sum = kvs[0:n, h, 0].reshape(n * BLK, HS)
        v_sum = kvs[0:n, h, 1].reshape(n * BLK, HS)
        k_two = [jnp.concatenate([kb[max(k - 1, 0)], kb[k]], axis=0) for k in range(GRP)]
        v_two = [jnp.concatenate([vb[max(k - 1, 0)], vb[k]], axis=0) for k in range(GRP)]
        lanes = [slice(k * BLK, (k + 1) * BLK) for k in range(GRP)]

        s_sum = dot_nt(k_sum, q_all).reshape(n, BLK, GRP * BLK)
        local = []
        for k in range(GRP):
            before = jnp.full((BLK, BLK), HIDDEN if k == 0 else 0.0, jnp.float32)
            mask = jnp.concatenate([before, own_bias], axis=0)
            local.append(dot_nt(k_two[k], q[k]) * scale_2 + mask)
        s_loc = jnp.concatenate(local, axis=1)
        hide = bias[half, 0:n]
        top_sum = jnp.max(s_sum, axis=1, keepdims=True) * scale_2 + hide
        top = jnp.maximum(jnp.max(top_sum, axis=0), jnp.max(s_loc, axis=0, keepdims=True))
        p_sum = jnp.exp2(s_sum * scale_2 + (hide - top[None])).reshape(n * BLK, GRP * BLK)
        p_loc = jnp.exp2(s_loc - top)
        total = jnp.sum(p_sum, axis=0, keepdims=True) + jnp.sum(p_loc, axis=0, keepdims=True)
        inv = 1.0 / total
        p_sum = p_sum * inv
        p_loc = p_loc * inv
        low_sum = p_sum.astype(jnp.bfloat16)
        low_loc = p_loc.astype(jnp.bfloat16)

        o_t = dot_tn(v_sum, low_sum) + jnp.concatenate(
            [dot_tn(v_two[k], low_loc[:, lanes[k]]) for k in range(GRP)], axis=1
        )
        o_t = o_t.astype(jnp.bfloat16).astype(jnp.float32)
        g_t = jnp.transpose(g_all.astype(jnp.float32))
        delta = jnp.sum(g_t * o_t, axis=0, keepdims=True)
        attended = jnp.transpose(o_t).astype(jnp.bfloat16)

        dp_sum = dot_nt(v_sum, g_all)
        dp_loc = jnp.concatenate([dot_nt(v_two[k], g[k]) for k in range(GRP)], axis=1)
        ds_sum = (p_sum * (dp_sum - delta)).astype(jnp.bfloat16)
        ds_loc = (p_loc * (dp_loc - delta)).astype(jnp.bfloat16)
        dq_t = dot_tn(k_sum, ds_sum) + jnp.concatenate(
            [dot_tn(k_two[k], ds_loc[:, lanes[k]]) for k in range(GRP)], axis=1
        )
        grad_q = (jnp.transpose(dq_t) * scale).astype(jnp.bfloat16)
        for k, (m, r) in enumerate(at):
            o_buf[m, h, r, :] = attended[lanes[k], :]
            dq_buf[m, h, r, :] = grad_q[lanes[k], :]

        dk_sum = (dot_nn(ds_sum, q_all) * scale).reshape(n, BLK, HS)
        dv_sum = dot_nn(low_sum, g_all).reshape(n, BLK, HS)
        dk_two = [dot_nn(ds_loc[:, lanes[k]], q[k]) * scale for k in range(GRP)]
        dv_two = [dot_nn(low_loc[:, lanes[k]], g[k]) for k in range(GRP)]
        for two, buf, kv in ((dk_two, dk_buf, 0), (dv_two, dv_buf, 1)):
            for k, (m, r) in enumerate(at):
                if k < GRP - 1:
                    buf[m, h, r, :] = (two[k][BLK:] + two[k + 1][:BLK]).astype(jnp.bfloat16)
                else:
                    last_acc[half, h, kv] = two[k][BLK:]
        return dk_sum, dv_sum

    outs = (o_out, dq_out, dk_out, dv_out)
    obufs = (o_buf, dq_buf, dk_buf, dv_buf)

    def grad_copy(s, h):
        return pltpu.make_async_remote_copy(
            src_ref=gstage.at[s, h],
            dst_ref=grecv.at[0 if s < groups else 1, group, h],
            send_sem=g_send.at[s, h],
            recv_sem=g_recv.at[0 if s < groups else 1, group, h],
            device_id={"ctx": (s if s < groups else spans - 1 - s) * GRP + member},
            device_id_type=MESH,
        )

    def send_out(a, src, rows, m, h):
        cols = pl.ds(pl.multiple_of((member * HG + h) * HS, HS), HS)

        @pl.when(member != m)
        def _():
            pltpu.make_async_remote_copy(
                src_ref=src,
                dst_ref=outs[a].at[rows, cols],
                send_sem=out_send.at[a],
                recv_sem=out_recv.at[a],
                device_id={"ctx": group * GRP + m},
                device_id_type=MESH,
            ).start()

        @pl.when(member == m)
        def _():
            pltpu.make_async_copy(src, outs[a].at[rows, cols], loc_out.at[a]).start()

    def finish_head(h):
        for which in range(2):
            span = group if which == 0 else spans - 1 - group
            for p in range(groups):

                @pl.when(needed(span, p, groups, every))
                def _():
                    ref = grecv.at[which, p, h]
                    pltpu.make_async_copy(ref, ref, g_recv.at[which, p, h]).wait()
                    last_acc[which, h] += grecv[which, p, h].astype(jnp.float32)

            late[which, h] = last_acc[which, h].astype(jnp.bfloat16)
            m = GRP - 1 if which == 0 else 0
            rows = pl.ds(which * BLK, BLK)
            for kv in range(2):
                send_out(2 + kv, late.at[which, h, kv], rows, m, h)

    def one_head(h, carry):
        n_low = groups - 1
        gather(h)
        dk_sum, dv_sum = one_span(0, n_low, h)
        sacc[0:n_low, 0] = dk_sum
        sacc[0:n_low, 1] = dv_sum
        dk_sum, dv_sum = one_span(1, slots, h)
        sacc[0:n_low, 0] += dk_sum[:n_low]
        sacc[0:n_low, 1] += dv_sum[:n_low]
        sacc[n_low:slots, 0] = dk_sum[n_low:]
        sacc[n_low:slots, 1] = dv_sum[n_low:]
        for s in range(slots):

            @pl.when(needed(s, group, groups, every))
            def _():
                gstage[s, h] = sacc[s].astype(jnp.bfloat16)
                grad_copy(s, h).start()

        last_acc[0, h] += sacc[group]
        for a in range(4):
            for m in range(GRP):
                if a < 2 or m in (1, 2):
                    rows = pl.ds(0, 2 * BLK)
                else:
                    rows = pl.ds(0 if m == 0 else BLK, BLK)
                send_out(a, obufs[a].at[m, h, rows, :], rows, m, h)

        @pl.when(h + 2 < HG)
        def _():
            spread(h + 2)

        @pl.when(h > 0)
        def _():
            finish_head(h - 1)

        return carry

    lax.fori_loop(0, HG, one_head, 0)

    finish_head(HG - 1)

    for a in range(4):
        away = (k_in, v_in, q_in, g_in)[a].at[:, pl.ds(0, (GRP - 1) * WID)]
        pltpu.make_async_copy(away, away, in_send.at[a]).wait()
    for p in range(groups):
        for which in range(2):
            for h in range(HG):
                wanted, copy = span_copy(which, p, h)

                @pl.when(wanted)
                def _():
                    copy.wait_send()

    for s in range(slots):

        @pl.when(needed(s, group, groups, every))
        def _():
            for h in range(HG):
                grad_copy(s, h).wait_send()

    for a in range(4):
        own = outs[a].at[:, pl.ds(0, WID)]
        away = outs[a].at[:, pl.ds(0, (GRP - 1) * WID)]
        pltpu.make_async_copy(own, own, loc_out.at[a]).wait()
        pltpu.make_async_copy(away, away, out_send.at[a]).wait()
        pltpu.make_async_copy(away, away, out_recv.at[a]).wait()


def place(*refs):
    sources, targets, sems = refs[:4], refs[4:8], refs[8]
    step = sources[0].shape[0] // PIECES
    copies = [
        pltpu.make_async_copy(
            sources[a].at[pl.ds(i * step, step)], targets[a].at[pl.ds(i * step, step)], sems.at[a, i]
        )
        for a in range(4)
        for i in range(PIECES)
    ]
    for copy in copies:
        copy.start()
    for copy in copies:
        copy.wait()


def on_device(queries, keys, values, grad_out, summary_lists):
    rows, width = queries.shape
    groups = lax.axis_size("ctx") // GRP
    every = groups * GRP * 2 // SUMS // GRP
    slots = 2 * groups - 1

    bf16, f32 = jnp.bfloat16, jnp.float32
    dma = pltpu.SemaphoreType.DMA
    anywhere = pl.BlockSpec(memory_space=pl.ANY)
    shapes = [jax.ShapeDtypeStruct((rows, width), bf16)] * 4
    results = pl.pallas_call(
        functools.partial(kernel, groups, every),
        out_shape=shapes,
        in_specs=[anywhere] * 4 + [pl.BlockSpec(memory_space=pltpu.SMEM)],
        out_specs=[anywhere] * 4,
        scratch_shapes=[
            pltpu.VMEM((GRP, HG, 2, 2, BLK, HS), bf16),
            pltpu.VMEM((GRP, HG, 2, rows, HS), bf16),
            pltpu.VMEM((slots, HG, 2, BLK, HS), bf16),
        ]
        + [pltpu.VMEM((GRP, HG, rows, HS), bf16)] * 4
        + [
            pltpu.VMEM((slots, 2, BLK, HS), f32),
            pltpu.VMEM((slots, HG, 2, BLK, HS), bf16),
            pltpu.VMEM((2, groups, HG, 2, BLK, HS), bf16),
            pltpu.VMEM((2, HG, 2, BLK, HS), f32),
            pltpu.VMEM((2, HG, 2, BLK, HS), bf16),
            pltpu.VMEM((2, slots, 1, GRP * BLK), f32),
            dma((4,)),
            dma((HG, GRP)),
            dma((HG, GRP)),
            dma((HG, GRP)),
            dma((HG,)),
            dma((HG,)),
            dma((2, groups, HG)),
            dma((slots, HG)),
            dma((slots, HG)),
            dma((2, groups, HG)),
            dma((4,)),
            dma((4,)),
            dma((4,)),
        ],
        compiler_params=pltpu.CompilerParams(
            collective_id=0, has_side_effects=True, vmem_limit_bytes=56 * 1024 * 1024
        ),
        cost_estimate=pl.CostEstimate(
            flops=6 * 10**9, bytes_accessed=8 * 10**6, transcendentals=3 * 10**6
        ),
    )(queries, keys, values, grad_out, summary_lists)
    return pl.pallas_call(
        place,
        out_shape=shapes,
        in_specs=[anywhere] * 4,
        out_specs=[anywhere] * 4,
        scratch_shapes=[dma((4, PIECES))],
        compiler_params=pltpu.CompilerParams(vmem_limit_bytes=60 * 1024 * 1024),
        cost_estimate=pl.CostEstimate(flops=0, bytes_accessed=6 * 10**6, transcendentals=0),
    )(*results)


def solution(mesh):
    rows = P(("dp", "ctx"), None)
    return jax.shard_map(
        on_device,
        mesh=mesh,
        in_specs=(rows, rows, rows, rows, P("dp", None)),
        out_specs=(rows, rows, rows, rows),
        check_vma=False,
    )
```

```python
import functools

import jax
import jax.numpy as jnp
from jax import lax
from jax.experimental import pallas as pl
from jax.experimental.pallas import tpu as pltpu
from jax.sharding import PartitionSpec as P

H = 12
HS = 128
BLK = 128
SUMS = 8
PICKS = 4
PIECES = 4
GRP = 4
HG = H // GRP
WID = HG * HS
HIDDEN = -1e30
LOG2_E = 1.4426950408889634
MESH = pl.DeviceIdType.MESH


def both(*terms):
    return functools.reduce(jnp.logical_and, terms)


def either(*terms):
    return functools.reduce(jnp.logical_or, terms)


def home(span, groups):
    return jnp.where(span < groups, span, 2 * groups - 1 - span)


def is_summary(span, every):
    return lax.rem(jnp.asarray(span + 1, jnp.int32), jnp.int32(every)) == 0


def needed(span, group, groups, every):
    span = jnp.asarray(span, jnp.int32)
    group = jnp.asarray(group, jnp.int32)
    return both(
        span <= 2 * groups - 2 - group,
        home(span, groups) != group,
        either(is_summary(span, every), span + 1 == group, span + 1 == 2 * groups - 1 - group),
    )


def dot_nn(a, b):
    return lax.dot_general(a, b, (((1,), (0,)), ((), ())), preferred_element_type=jnp.float32)


def member_rows(half, k):
    return (k, slice(0, BLK)) if half == 0 else (GRP - 1 - k, slice(BLK, 2 * BLK))


def kernel(
    groups,
    every,
    q_in, k_in, v_in, g_in, lists,
    o_out, dq_out, dk_out, dv_out,
    kv_buf, qg_buf, kvs,
    o_buf, dq_buf, dk_buf, dv_buf,
    sacc, gstage, grecv, last_acc, late,
    bias, in_send, first_recv, rest_recv, qg_recv, loc_kv, loc_qg,
    z_send, z_recv, g_send, g_recv, out_send, out_recv, loc_out,
):
    spans = 2 * groups
    slots = spans - 1
    here = lax.axis_index("ctx")
    group = here // GRP
    member = lax.rem(here, GRP)
    scale = HS ** (-0.5)
    scale_2 = scale * LOG2_E

    barrier = pltpu.get_barrier_semaphore()
    for off in range(1, GRP):
        peer = group * GRP + lax.rem(member + off, GRP)
        pl.semaphore_signal(barrier, inc=1, device_id={"ctx": peer}, device_id_type=MESH)
    for off in range(1, groups):
        peer = lax.rem(group + off, groups) * GRP + member
        pl.semaphore_signal(barrier, inc=1, device_id={"ctx": peer}, device_id_type=MESH)

    def head_cols(m, h):
        return pl.ds(pl.multiple_of((m * HG + h) * HS, HS), HS)

    for h in range(HG):
        cols = head_cols(member, h)
        for half in range(2):
            rows = pl.ds(half * BLK, BLK)
            for kv, ref in enumerate((k_in, v_in)):
                pltpu.make_async_copy(
                    ref.at[rows, cols], kv_buf.at[member, h, half, kv], loc_kv.at[h]
                ).start()
        for i, ref in enumerate((q_in, g_in)):
            pltpu.make_async_copy(ref.at[:, cols], qg_buf.at[member, h, i], loc_qg.at[h]).start()
    for s in range(slots):

        @pl.when(both(jnp.logical_not(needed(s, group, groups, every)), group != s))
        def _():
            kvs[s] = jnp.zeros(kvs.shape[1:], kvs.dtype)

    pl.semaphore_wait(barrier, GRP - 1 + groups - 1)

    front = jnp.where(member < 2, 1, 0)

    def send_kv(h, half, recv):
        rows = pl.ds(pl.multiple_of(half * BLK, BLK), BLK)
        for m in range(GRP):

            @pl.when(member != m)
            def _():
                for kv, ref in enumerate((k_in, v_in)):
                    pltpu.make_async_remote_copy(
                        src_ref=ref.at[rows, head_cols(m, h)],
                        dst_ref=kv_buf.at[member, h, half, kv],
                        send_sem=in_send.at[kv],
                        recv_sem=recv.at[h, member],
                        device_id={"ctx": group * GRP + m},
                        device_id_type=MESH,
                    ).start()

    def send_qg(h):
        for m in range(GRP):

            @pl.when(member != m)
            def _():
                for i, ref in enumerate((q_in, g_in)):
                    pltpu.make_async_remote_copy(
                        src_ref=ref.at[:, head_cols(m, h)],
                        dst_ref=qg_buf.at[member, h, i],
                        send_sem=in_send.at[2 + i],
                        recv_sem=qg_recv.at[h, member],
                        device_id={"ctx": group * GRP + m},
                        device_id_type=MESH,
                    ).start()

    send_kv(0, front, first_recv)
    send_kv(1, front, first_recv)
    send_kv(0, 1 - front, rest_recv)
    send_qg(0)
    for h in range(1, HG):
        if h + 1 < HG:
            send_kv(h + 1, front, first_recv)
        send_kv(h, 1 - front, rest_recv)
        send_qg(h)

    def span_copy(which, p, h):
        span = group if which == 0 else spans - 1 - group
        m = GRP - 1 if which == 0 else 0
        slot = jnp.minimum(span, slots - 1)
        return needed(span, p, groups, every), pltpu.make_async_remote_copy(
            src_ref=kv_buf.at[m, h, which],
            dst_ref=kvs.at[slot, h],
            send_sem=z_send.at[which, p, h],
            recv_sem=z_recv.at[slot, h],
            device_id={"ctx": p * GRP + member},
            device_id_type=MESH,
        )

    def spread(h):
        mine = kv_buf.at[member, h]
        pltpu.make_async_copy(mine, mine, loc_kv.at[h]).wait()
        for m in range(GRP):

            @pl.when(member != m)
            def _():
                ref = kv_buf.at[m, h, 1 if m < 2 else 0]
                pltpu.make_async_copy(ref, ref, first_recv.at[h, m]).wait()

        for p in range(groups):
            for which in range(2):
                wanted, copy = span_copy(which, p, h)

                @pl.when(wanted)
                def _():
                    copy.start()

        kvs[group, h] = kv_buf[GRP - 1, h, 0]

    def gather(h):
        mine = qg_buf.at[member, h]
        pltpu.make_async_copy(mine, mine, loc_qg.at[h]).wait()
        for m in range(GRP):

            @pl.when(member != m)
            def _():
                ref = kv_buf.at[m, h, 0 if m < 2 else 1]
                pltpu.make_async_copy(ref, ref, rest_recv.at[h, m]).wait()
                ref = qg_buf.at[m, h]
                pltpu.make_async_copy(ref, ref, qg_recv.at[h, m]).wait()

        for s in range(slots):

            @pl.when(needed(s, group, groups, every))
            def _():
                pltpu.make_async_copy(kvs.at[s, h], kvs.at[s, h], z_recv.at[s, h]).wait()

    for half in range(2):
        for k in range(GRP):
            block = (group if half == 0 else spans - 1 - group) * GRP + k
            picks = [lists[block, i] for i in range(PICKS)]
            for s in range(slots):
                end = s * GRP + GRP - 1
                seen = end == block - 1
                if (s + 1) % every == 0:
                    picked = either(*[pick == (s + 1) // every - 1 for pick in picks])
                    seen = either(seen, both(picked, end < block - 1))
                row = jnp.full((1, BLK), jnp.where(seen, 0.0, HIDDEN), jnp.float32)
                bias[half, s, :, k * BLK : (k + 1) * BLK] = row

    spread(0)
    spread(1)

    key_at = lax.broadcasted_iota(jnp.int32, (BLK, BLK), 0)
    query_at = lax.broadcasted_iota(jnp.int32, (BLK, BLK), 1)
    own_bias = jnp.where(key_at <= query_at, 0.0, HIDDEN).astype(jnp.float32)

    def one_span(half, n, h, k_sum, v_sum, k_sum_t, v_sum_t):
        at = [member_rows(half, k) for k in range(GRP)]
        q = [qg_buf[m, h, 0, r, :] for m, r in at]
        g = [qg_buf[m, h, 1, r, :] for m, r in at]
        kb = [kv_buf[m, h, half, 0] for m, r in at]
        vb = [kv_buf[m, h, half, 1] for m, r in at]
        q_all = jnp.concatenate(q, axis=0)
        g_all = jnp.concatenate(g, axis=0)
        q_t = jnp.transpose(q_all)
        g_t = jnp.transpose(g_all)
        k_two = [jnp.concatenate([kb[max(k - 1, 0)], kb[k]], axis=0) for k in range(GRP)]
        v_two = [jnp.concatenate([vb[max(k - 1, 0)], vb[k]], axis=0) for k in range(GRP)]
        kb_t = [jnp.transpose(block) for block in kb]
        vb_t = [jnp.transpose(block) for block in vb]
        k_two_t = [jnp.concatenate([kb_t[max(k - 1, 0)], kb_t[k]], axis=1) for k in range(GRP)]
        v_two_t = [jnp.concatenate([vb_t[max(k - 1, 0)], vb_t[k]], axis=1) for k in range(GRP)]
        lanes = [slice(k * BLK, (k + 1) * BLK) for k in range(GRP)]

        s_sum = dot_nn(k_sum, q_t).reshape(n, BLK, GRP * BLK)
        local = []
        for k in range(GRP):
            before = jnp.full((BLK, BLK), HIDDEN if k == 0 else 0.0, jnp.float32)
            mask = jnp.concatenate([before, own_bias], axis=0)
            local.append(dot_nn(k_two[k], q_t[:, lanes[k]]) * scale_2 + mask)
        s_loc = jnp.concatenate(local, axis=1)
        hide = bias[half, 0:n]
        top_sum = jnp.max(s_sum, axis=1, keepdims=True) * scale_2 + hide
        top = jnp.maximum(jnp.max(top_sum, axis=0), jnp.max(s_loc, axis=0, keepdims=True))
        p_sum = jnp.exp2(s_sum * scale_2 + (hide - top[None])).reshape(n * BLK, GRP * BLK)
        p_loc = jnp.exp2(s_loc - top)
        total = jnp.sum(p_sum, axis=0, keepdims=True) + jnp.sum(p_loc, axis=0, keepdims=True)
        inv = 1.0 / total
        p_sum = p_sum * inv
        p_loc = p_loc * inv
        low_sum = p_sum.astype(jnp.bfloat16)
        low_loc = p_loc.astype(jnp.bfloat16)

        o_t = dot_nn(v_sum_t, low_sum) + jnp.concatenate(
            [dot_nn(v_two_t[k], low_loc[:, lanes[k]]) for k in range(GRP)], axis=1
        )
        o_t = o_t.astype(jnp.bfloat16)
        delta = jnp.sum(
            g_t.astype(jnp.float32) * o_t.astype(jnp.float32), axis=0, keepdims=True
        )
        attended = jnp.transpose(o_t)

        dp_sum = dot_nn(v_sum, g_t)
        dp_loc = jnp.concatenate([dot_nn(v_two[k], g_t[:, lanes[k]]) for k in range(GRP)], axis=1)
        ds_sum = (p_sum * (dp_sum - delta)).astype(jnp.bfloat16)
        ds_loc = (p_loc * (dp_loc - delta)).astype(jnp.bfloat16)
        dq_t = dot_nn(k_sum_t, ds_sum) + jnp.concatenate(
            [dot_nn(k_two_t[k], ds_loc[:, lanes[k]]) for k in range(GRP)], axis=1
        )
        grad_q = jnp.transpose((dq_t * scale).astype(jnp.bfloat16))
        for k, (m, r) in enumerate(at):
            o_buf[m, h, r, :] = attended[lanes[k], :]
            dq_buf[m, h, r, :] = grad_q[lanes[k], :]

        dk_sum = (dot_nn(ds_sum, q_all) * scale).reshape(n, BLK, HS)
        dv_sum = dot_nn(low_sum, g_all).reshape(n, BLK, HS)
        dk_two = [dot_nn(ds_loc[:, lanes[k]], q[k]) * scale for k in range(GRP)]
        dv_two = [dot_nn(low_loc[:, lanes[k]], g[k]) for k in range(GRP)]
        for two, buf, kv in ((dk_two, dk_buf, 0), (dv_two, dv_buf, 1)):
            for k, (m, r) in enumerate(at):
                if k < GRP - 1:
                    buf[m, h, r, :] = (two[k][BLK:] + two[k + 1][:BLK]).astype(jnp.bfloat16)
                else:
                    last_acc[half, h, kv] = two[k][BLK:]
        return dk_sum, dv_sum

    outs = (o_out, dq_out, dk_out, dv_out)
    obufs = (o_buf, dq_buf, dk_buf, dv_buf)

    def grad_copy(s, h):
        return pltpu.make_async_remote_copy(
            src_ref=gstage.at[s, h],
            dst_ref=grecv.at[0 if s < groups else 1, group, h],
            send_sem=g_send.at[s, h],
            recv_sem=g_recv.at[0 if s < groups else 1, group, h],
            device_id={"ctx": (s if s < groups else spans - 1 - s) * GRP + member},
            device_id_type=MESH,
        )

    def send_out(a, src, rows, m, h):
        cols = pl.ds(pl.multiple_of((member * HG + h) * HS, HS), HS)

        @pl.when(member != m)
        def _():
            pltpu.make_async_remote_copy(
                src_ref=src,
                dst_ref=outs[a].at[rows, cols],
                send_sem=out_send.at[a],
                recv_sem=out_recv.at[a],
                device_id={"ctx": group * GRP + m},
                device_id_type=MESH,
            ).start()

        @pl.when(member == m)
        def _():
            pltpu.make_async_copy(src, outs[a].at[rows, cols], loc_out.at[a]).start()

    def finish_head(h):
        for which in range(2):
            span = group if which == 0 else spans - 1 - group
            for p in range(groups):

                @pl.when(needed(span, p, groups, every))
                def _():
                    ref = grecv.at[which, p, h]
                    pltpu.make_async_copy(ref, ref, g_recv.at[which, p, h]).wait()
                    last_acc[which, h] += grecv[which, p, h].astype(jnp.float32)

            late[which, h] = last_acc[which, h].astype(jnp.bfloat16)
            m = GRP - 1 if which == 0 else 0
            rows = pl.ds(which * BLK, BLK)
            for kv in range(2):
                send_out(2 + kv, late.at[which, h, kv], rows, m, h)

    def one_head(h, carry):
        n_low = groups - 1
        gather(h)
        k_sum = kvs[0:slots, h, 0].reshape(slots * BLK, HS)
        v_sum = kvs[0:slots, h, 1].reshape(slots * BLK, HS)
        k_sum_t = jnp.transpose(k_sum)
        v_sum_t = jnp.transpose(v_sum)

        def ship(first, end):
            for s in range(first, end):

                @pl.when(needed(s, group, groups, every))
                def _():
                    gstage[s, h] = sacc[s].astype(jnp.bfloat16)
                    grad_copy(s, h).start()

        dk_sum, dv_sum = one_span(1, slots, h, k_sum, v_sum, k_sum_t, v_sum_t)
        sacc[:, 0] = dk_sum
        sacc[:, 1] = dv_sum
        ship(n_low, slots)
        low = n_low * BLK
        dk_sum, dv_sum = one_span(
            0, n_low, h, k_sum[:low], v_sum[:low], k_sum_t[:, :low], v_sum_t[:, :low]
        )
        sacc[0:n_low, 0] += dk_sum
        sacc[0:n_low, 1] += dv_sum
        ship(0, n_low)
        last_acc[0, h] += sacc[group]
        for a in range(4):
            for m in range(GRP):
                if a < 2 or m in (1, 2):
                    rows = pl.ds(0, 2 * BLK)
                else:
                    rows = pl.ds(0 if m == 0 else BLK, BLK)
                send_out(a, obufs[a].at[m, h, rows, :], rows, m, h)

        @pl.when(h + 2 < HG)
        def _():
            spread(h + 2)

        @pl.when(h > 0)
        def _():
            finish_head(h - 1)

        return carry

    lax.fori_loop(0, HG, one_head, 0)

    finish_head(HG - 1)

    for a in range(4):
        away = (k_in, v_in, q_in, g_in)[a].at[:, pl.ds(0, (GRP - 1) * WID)]
        pltpu.make_async_copy(away, away, in_send.at[a]).wait()
    for p in range(groups):
        for which in range(2):
            for h in range(HG):
                wanted, copy = span_copy(which, p, h)

                @pl.when(wanted)
                def _():
                    copy.wait_send()

    for s in range(slots):

        @pl.when(needed(s, group, groups, every))
        def _():
            for h in range(HG):
                grad_copy(s, h).wait_send()

    for a in range(4):
        own = outs[a].at[:, pl.ds(0, WID)]
        away = outs[a].at[:, pl.ds(0, (GRP - 1) * WID)]
        pltpu.make_async_copy(own, own, loc_out.at[a]).wait()
        pltpu.make_async_copy(away, away, out_send.at[a]).wait()
        pltpu.make_async_copy(away, away, out_recv.at[a]).wait()


def place(*refs):
    sources, targets, held, arrive, leave = refs[:4], refs[4:8], refs[8], refs[9], refs[10]
    step = sources[0].shape[0] // PIECES
    pairs = []
    for a in range(4):
        for i in range(PIECES):
            rows = pl.ds(i * step, step)
            mid = held.at[a, rows]
            pairs.append(
                (
                    pltpu.make_async_copy(sources[a].at[rows], mid, arrive.at[a, i]),
                    pltpu.make_async_copy(mid, targets[a].at[rows], leave.at[a, i]),
                )
            )
    for load, _ in pairs:
        load.start()
    for load, store in pairs:
        load.wait()
        store.start()
    for _, store in pairs:
        store.wait()


def on_device(queries, keys, values, grad_out, summary_lists):
    rows, width = queries.shape
    groups = lax.axis_size("ctx") // GRP
    every = groups * GRP * 2 // SUMS // GRP
    slots = 2 * groups - 1

    bf16, f32 = jnp.bfloat16, jnp.float32
    dma = pltpu.SemaphoreType.DMA
    anywhere = pl.BlockSpec(memory_space=pl.ANY)
    shapes = [jax.ShapeDtypeStruct((rows, width), bf16)] * 4
    results = pl.pallas_call(
        functools.partial(kernel, groups, every),
        out_shape=shapes,
        in_specs=[anywhere] * 4 + [pl.BlockSpec(memory_space=pltpu.SMEM)],
        out_specs=[anywhere] * 4,
        scratch_shapes=[
            pltpu.VMEM((GRP, HG, 2, 2, BLK, HS), bf16),
            pltpu.VMEM((GRP, HG, 2, rows, HS), bf16),
            pltpu.VMEM((slots, HG, 2, BLK, HS), bf16),
        ]
        + [pltpu.VMEM((GRP, HG, rows, HS), bf16)] * 4
        + [
            pltpu.VMEM((slots, 2, BLK, HS), f32),
            pltpu.VMEM((slots, HG, 2, BLK, HS), bf16),
            pltpu.VMEM((2, groups, HG, 2, BLK, HS), bf16),
            pltpu.VMEM((2, HG, 2, BLK, HS), f32),
            pltpu.VMEM((2, HG, 2, BLK, HS), bf16),
            pltpu.VMEM((2, slots, 1, GRP * BLK), f32),
            dma((4,)),
            dma((HG, GRP)),
            dma((HG, GRP)),
            dma((HG, GRP)),
            dma((HG,)),
            dma((HG,)),
            dma((2, groups, HG)),
            dma((slots, HG)),
            dma((slots, HG)),
            dma((2, groups, HG)),
            dma((4,)),
            dma((4,)),
            dma((4,)),
        ],
        compiler_params=pltpu.CompilerParams(
            collective_id=0, has_side_effects=True, vmem_limit_bytes=56 * 1024 * 1024
        ),
        cost_estimate=pl.CostEstimate(
            flops=6 * 10**9, bytes_accessed=8 * 10**6, transcendentals=3 * 10**6
        ),
    )(queries, keys, values, grad_out, summary_lists)
    return pl.pallas_call(
        place,
        out_shape=shapes,
        in_specs=[anywhere] * 4,
        out_specs=[anywhere] * 4,
        scratch_shapes=[pltpu.VMEM((4, rows, width), bf16), dma((4, PIECES)), dma((4, PIECES))],
        compiler_params=pltpu.CompilerParams(vmem_limit_bytes=60 * 1024 * 1024),
        cost_estimate=pl.CostEstimate(flops=0, bytes_accessed=6 * 10**6, transcendentals=0),
    )(*results)


def solution(mesh):
    rows = P(("dp", "ctx"), None)
    return jax.shard_map(
        on_device,
        mesh=mesh,
        in_specs=(rows, rows, rows, rows, P("dp", None)),
        out_specs=(rows, rows, rows, rows),
        check_vma=False,
    )
```

```python
import functools

import jax
import jax.numpy as jnp
from jax import lax
from jax.experimental import pallas as pl
from jax.experimental.pallas import tpu as pltpu
from jax.sharding import PartitionSpec as P

H = 12
HS = 128
BLK = 128
SUMS = 8
PICKS = 4
PIECES = 4
GRP = 4
HG = H // GRP
WID = HG * HS
HIDDEN = -1e30
LOG2_E = 1.4426950408889634
MESH = pl.DeviceIdType.MESH


def both(*terms):
    return functools.reduce(jnp.logical_and, terms)


def either(*terms):
    return functools.reduce(jnp.logical_or, terms)


def home(span, groups):
    return jnp.where(span < groups, span, 2 * groups - 1 - span)


def is_summary(span, every):
    return lax.rem(jnp.asarray(span + 1, jnp.int32), jnp.int32(every)) == 0


def needed(span, group, groups, every):
    span = jnp.asarray(span, jnp.int32)
    group = jnp.asarray(group, jnp.int32)
    return both(
        span <= 2 * groups - 2 - group,
        home(span, groups) != group,
        either(is_summary(span, every), span + 1 == group, span + 1 == 2 * groups - 1 - group),
    )


def dot_nn(a, b):
    return lax.dot_general(a, b, (((1,), (0,)), ((), ())), preferred_element_type=jnp.float32)


def member_rows(half, k):
    return (k, slice(0, BLK)) if half == 0 else (GRP - 1 - k, slice(BLK, 2 * BLK))


def kernel(
    groups,
    every,
    q_in, k_in, v_in, g_in, lists,
    o_out, dq_out, dk_out, dv_out,
    kv_buf, qg_buf, kvs,
    o_buf, dq_buf, dk_buf, dv_buf,
    sacc, gstage, grecv, last_acc, late,
    bias, in_send, first_recv, rest_recv, qg_recv, loc_kv, loc_qg,
    z_send, z_recv, g_send, g_recv, out_send, out_recv, loc_out,
):
    spans = 2 * groups
    slots = spans - 1
    here = lax.axis_index("ctx")
    group = here // GRP
    member = lax.rem(here, GRP)
    scale = HS ** (-0.5)
    scale_2 = scale * LOG2_E

    barrier = pltpu.get_barrier_semaphore()
    for off in range(1, GRP):
        peer = group * GRP + lax.rem(member + off, GRP)
        pl.semaphore_signal(barrier, inc=1, device_id={"ctx": peer}, device_id_type=MESH)
    for off in range(1, groups):
        peer = lax.rem(group + off, groups) * GRP + member
        pl.semaphore_signal(barrier, inc=1, device_id={"ctx": peer}, device_id_type=MESH)

    def head_cols(m, h):
        return pl.ds(pl.multiple_of((m * HG + h) * HS, HS), HS)

    for h in range(HG):
        cols = head_cols(member, h)
        for half in range(2):
            rows = pl.ds(half * BLK, BLK)
            for kv, ref in enumerate((k_in, v_in)):
                pltpu.make_async_copy(
                    ref.at[rows, cols], kv_buf.at[member, h, half, kv], loc_kv.at[h]
                ).start()
        for i, ref in enumerate((q_in, g_in)):
            pltpu.make_async_copy(ref.at[:, cols], qg_buf.at[member, h, i], loc_qg.at[h]).start()
    for s in range(slots):

        @pl.when(both(jnp.logical_not(needed(s, group, groups, every)), group != s))
        def _():
            kvs[s] = jnp.zeros(kvs.shape[1:], kvs.dtype)

    pl.semaphore_wait(barrier, GRP - 1 + groups - 1)

    front = jnp.where(member < 2, 1, 0)

    def send_kv(h, half, recv):
        rows = pl.ds(pl.multiple_of(half * BLK, BLK), BLK)
        for m in range(GRP):

            @pl.when(member != m)
            def _():
                for kv, ref in enumerate((k_in, v_in)):
                    pltpu.make_async_remote_copy(
                        src_ref=ref.at[rows, head_cols(m, h)],
                        dst_ref=kv_buf.at[member, h, half, kv],
                        send_sem=in_send.at[kv],
                        recv_sem=recv.at[h, member],
                        device_id={"ctx": group * GRP + m},
                        device_id_type=MESH,
                    ).start()

    def send_qg(h):
        for m in range(GRP):

            @pl.when(member != m)
            def _():
                for i, ref in enumerate((q_in, g_in)):
                    pltpu.make_async_remote_copy(
                        src_ref=ref.at[:, head_cols(m, h)],
                        dst_ref=qg_buf.at[member, h, i],
                        send_sem=in_send.at[2 + i],
                        recv_sem=qg_recv.at[h, member],
                        device_id={"ctx": group * GRP + m},
                        device_id_type=MESH,
                    ).start()

    send_kv(0, front, first_recv)
    send_kv(0, 1 - front, rest_recv)
    send_qg(0)
    send_kv(1, front, first_recv)

    def span_copy(which, p, h):
        span = group if which == 0 else spans - 1 - group
        m = GRP - 1 if which == 0 else 0
        slot = jnp.minimum(span, slots - 1)
        return needed(span, p, groups, every), pltpu.make_async_remote_copy(
            src_ref=kv_buf.at[m, h, which],
            dst_ref=kvs.at[slot, h],
            send_sem=z_send.at[which, p, h],
            recv_sem=z_recv.at[slot, h],
            device_id={"ctx": p * GRP + member},
            device_id_type=MESH,
        )

    def spread(h):
        mine = kv_buf.at[member, h]
        pltpu.make_async_copy(mine, mine, loc_kv.at[h]).wait()
        for m in range(GRP):

            @pl.when(member != m)
            def _():
                ref = kv_buf.at[m, h, 1 if m < 2 else 0]
                pltpu.make_async_copy(ref, ref, first_recv.at[h, m]).wait()

        for p in range(groups):
            for which in range(2):
                wanted, copy = span_copy(which, p, h)

                @pl.when(wanted)
                def _():
                    copy.start()

        kvs[group, h] = kv_buf[GRP - 1, h, 0]

    def gather(h):
        mine = qg_buf.at[member, h]
        pltpu.make_async_copy(mine, mine, loc_qg.at[h]).wait()
        for m in range(GRP):

            @pl.when(member != m)
            def _():
                ref = kv_buf.at[m, h, 0 if m < 2 else 1]
                pltpu.make_async_copy(ref, ref, rest_recv.at[h, m]).wait()
                ref = qg_buf.at[m, h]
                pltpu.make_async_copy(ref, ref, qg_recv.at[h, m]).wait()

        for s in range(slots):

            @pl.when(needed(s, group, groups, every))
            def _():
                pltpu.make_async_copy(kvs.at[s, h], kvs.at[s, h], z_recv.at[s, h]).wait()

    for half in range(2):
        for k in range(GRP):
            block = (group if half == 0 else spans - 1 - group) * GRP + k
            picks = [lists[block, i] for i in range(PICKS)]
            for s in range(slots):
                end = s * GRP + GRP - 1
                seen = end == block - 1
                if (s + 1) % every == 0:
                    picked = either(*[pick == (s + 1) // every - 1 for pick in picks])
                    seen = either(seen, both(picked, end < block - 1))
                row = jnp.full((1, BLK), jnp.where(seen, 0.0, HIDDEN), jnp.float32)
                bias[half, s, :, k * BLK : (k + 1) * BLK] = row

    spread(0)
    send_kv(1, 1 - front, rest_recv)

    key_at = lax.broadcasted_iota(jnp.int32, (BLK, BLK), 0)
    query_at = lax.broadcasted_iota(jnp.int32, (BLK, BLK), 1)
    own_bias = jnp.where(key_at <= query_at, 0.0, HIDDEN).astype(jnp.float32)

    def one_span(half, n, h, k_sum, v_sum, k_sum_t, v_sum_t):
        at = [member_rows(half, k) for k in range(GRP)]
        q = [qg_buf[m, h, 0, r, :] for m, r in at]
        g = [qg_buf[m, h, 1, r, :] for m, r in at]
        kb = [kv_buf[m, h, half, 0] for m, r in at]
        vb = [kv_buf[m, h, half, 1] for m, r in at]
        q_all = jnp.concatenate(q, axis=0)
        g_all = jnp.concatenate(g, axis=0)
        q_t = jnp.transpose(q_all)
        g_t = jnp.transpose(g_all)
        k_two = [jnp.concatenate([kb[max(k - 1, 0)], kb[k]], axis=0) for k in range(GRP)]
        v_two = [jnp.concatenate([vb[max(k - 1, 0)], vb[k]], axis=0) for k in range(GRP)]
        kb_t = [jnp.transpose(block) for block in kb]
        vb_t = [jnp.transpose(block) for block in vb]
        k_two_t = [jnp.concatenate([kb_t[max(k - 1, 0)], kb_t[k]], axis=1) for k in range(GRP)]
        v_two_t = [jnp.concatenate([vb_t[max(k - 1, 0)], vb_t[k]], axis=1) for k in range(GRP)]
        lanes = [slice(k * BLK, (k + 1) * BLK) for k in range(GRP)]

        s_sum = dot_nn(k_sum, q_t).reshape(n, BLK, GRP * BLK)
        local = []
        for k in range(GRP):
            before = jnp.full((BLK, BLK), HIDDEN if k == 0 else 0.0, jnp.float32)
            mask = jnp.concatenate([before, own_bias], axis=0)
            local.append(dot_nn(k_two[k], q_t[:, lanes[k]]) * scale_2 + mask)
        s_loc = jnp.concatenate(local, axis=1)
        hide = bias[half, 0:n]
        top_sum = jnp.max(s_sum, axis=1, keepdims=True) * scale_2 + hide
        top = jnp.maximum(jnp.max(top_sum, axis=0), jnp.max(s_loc, axis=0, keepdims=True))
        p_sum = jnp.exp2(s_sum * scale_2 + (hide - top[None])).reshape(n * BLK, GRP * BLK)
        p_loc = jnp.exp2(s_loc - top)
        total = jnp.sum(p_sum, axis=0, keepdims=True) + jnp.sum(p_loc, axis=0, keepdims=True)
        inv = 1.0 / total
        p_sum = p_sum * inv
        p_loc = p_loc * inv
        low_sum = p_sum.astype(jnp.bfloat16)
        low_loc = p_loc.astype(jnp.bfloat16)

        o_t = dot_nn(v_sum_t, low_sum) + jnp.concatenate(
            [dot_nn(v_two_t[k], low_loc[:, lanes[k]]) for k in range(GRP)], axis=1
        )
        o_t = o_t.astype(jnp.bfloat16)
        delta = jnp.sum(
            g_t.astype(jnp.float32) * o_t.astype(jnp.float32), axis=0, keepdims=True
        )
        attended = jnp.transpose(o_t)

        dp_sum = dot_nn(v_sum, g_t)
        dp_loc = jnp.concatenate([dot_nn(v_two[k], g_t[:, lanes[k]]) for k in range(GRP)], axis=1)
        ds_sum = (p_sum * (dp_sum - delta)).astype(jnp.bfloat16)
        ds_loc = (p_loc * (dp_loc - delta)).astype(jnp.bfloat16)
        dq_t = dot_nn(k_sum_t, ds_sum) + jnp.concatenate(
            [dot_nn(k_two_t[k], ds_loc[:, lanes[k]]) for k in range(GRP)], axis=1
        )
        grad_q = jnp.transpose((dq_t * scale).astype(jnp.bfloat16))
        for k, (m, r) in enumerate(at):
            o_buf[m, h, r, :] = attended[lanes[k], :]
            dq_buf[m, h, r, :] = grad_q[lanes[k], :]

        dk_sum = (dot_nn(ds_sum, q_all) * scale).reshape(n, BLK, HS)
        dv_sum = dot_nn(low_sum, g_all).reshape(n, BLK, HS)
        dk_two = [dot_nn(ds_loc[:, lanes[k]], q[k]) * scale for k in range(GRP)]
        dv_two = [dot_nn(low_loc[:, lanes[k]], g[k]) for k in range(GRP)]
        for two, buf, kv in ((dk_two, dk_buf, 0), (dv_two, dv_buf, 1)):
            for k, (m, r) in enumerate(at):
                if k < GRP - 1:
                    buf[m, h, r, :] = (two[k][BLK:] + two[k + 1][:BLK]).astype(jnp.bfloat16)
                else:
                    last_acc[half, h, kv] = two[k][BLK:]
        return dk_sum, dv_sum

    outs = (o_out, dq_out, dk_out, dv_out)
    obufs = (o_buf, dq_buf, dk_buf, dv_buf)

    def grad_copy(s, h):
        return pltpu.make_async_remote_copy(
            src_ref=gstage.at[s, h],
            dst_ref=grecv.at[0 if s < groups else 1, group, h],
            send_sem=g_send.at[s, h],
            recv_sem=g_recv.at[0 if s < groups else 1, group, h],
            device_id={"ctx": (s if s < groups else spans - 1 - s) * GRP + member},
            device_id_type=MESH,
        )

    def send_out(a, src, rows, m, h):
        cols = pl.ds(pl.multiple_of((member * HG + h) * HS, HS), HS)

        @pl.when(member != m)
        def _():
            pltpu.make_async_remote_copy(
                src_ref=src,
                dst_ref=outs[a].at[rows, cols],
                send_sem=out_send.at[a],
                recv_sem=out_recv.at[a],
                device_id={"ctx": group * GRP + m},
                device_id_type=MESH,
            ).start()

        @pl.when(member == m)
        def _():
            pltpu.make_async_copy(src, outs[a].at[rows, cols], loc_out.at[a]).start()

    def finish_head(h):
        for which in range(2):
            span = group if which == 0 else spans - 1 - group
            for p in range(groups):

                @pl.when(needed(span, p, groups, every))
                def _():
                    ref = grecv.at[which, p, h]
                    pltpu.make_async_copy(ref, ref, g_recv.at[which, p, h]).wait()
                    last_acc[which, h] += grecv[which, p, h].astype(jnp.float32)

            late[which, h] = last_acc[which, h].astype(jnp.bfloat16)
            m = GRP - 1 if which == 0 else 0
            rows = pl.ds(which * BLK, BLK)
            for kv in range(2):
                send_out(2 + kv, late.at[which, h, kv], rows, m, h)

    def one_head(h, carry):
        n_low = groups - 1
        gather(h)

        @pl.when(h + 1 < HG)
        def _():
            send_qg(h + 1)

            @pl.when(h + 2 < HG)
            def _():
                send_kv(h + 2, front, first_recv)

            spread(h + 1)

        k_sum = kvs[0:slots, h, 0].reshape(slots * BLK, HS)
        v_sum = kvs[0:slots, h, 1].reshape(slots * BLK, HS)
        k_sum_t = jnp.transpose(k_sum)
        v_sum_t = jnp.transpose(v_sum)

        def ship(first, end):
            for s in range(first, end):

                @pl.when(needed(s, group, groups, every))
                def _():
                    gstage[s, h] = sacc[s].astype(jnp.bfloat16)
                    grad_copy(s, h).start()

        dk_sum, dv_sum = one_span(1, slots, h, k_sum, v_sum, k_sum_t, v_sum_t)
        sacc[:, 0] = dk_sum
        sacc[:, 1] = dv_sum
        ship(n_low, slots)
        low = n_low * BLK
        dk_sum, dv_sum = one_span(
            0, n_low, h, k_sum[:low], v_sum[:low], k_sum_t[:, :low], v_sum_t[:, :low]
        )
        sacc[0:n_low, 0] += dk_sum
        sacc[0:n_low, 1] += dv_sum
        ship(0, n_low)
        last_acc[0, h] += sacc[group]
        for a in range(4):
            for m in range(GRP):
                if a < 2 or m in (1, 2):
                    rows = pl.ds(0, 2 * BLK)
                else:
                    rows = pl.ds(0 if m == 0 else BLK, BLK)
                send_out(a, obufs[a].at[m, h, rows, :], rows, m, h)

        @pl.when(h + 2 < HG)
        def _():
            send_kv(h + 2, 1 - front, rest_recv)

        @pl.when(h > 0)
        def _():
            finish_head(h - 1)

        return carry

    lax.fori_loop(0, HG, one_head, 0)

    finish_head(HG - 1)

    for a in range(4):
        away = (k_in, v_in, q_in, g_in)[a].at[:, pl.ds(0, (GRP - 1) * WID)]
        pltpu.make_async_copy(away, away, in_send.at[a]).wait()
    for p in range(groups):
        for which in range(2):
            for h in range(HG):
                wanted, copy = span_copy(which, p, h)

                @pl.when(wanted)
                def _():
                    copy.wait_send()

    for s in range(slots):

        @pl.when(needed(s, group, groups, every))
        def _():
            for h in range(HG):
                grad_copy(s, h).wait_send()

    for a in range(4):
        own = outs[a].at[:, pl.ds(0, WID)]
        away = outs[a].at[:, pl.ds(0, (GRP - 1) * WID)]
        pltpu.make_async_copy(own, own, loc_out.at[a]).wait()
        pltpu.make_async_copy(away, away, out_send.at[a]).wait()
        pltpu.make_async_copy(away, away, out_recv.at[a]).wait()


def place(*refs):
    sources, targets, held, arrive, leave = refs[:4], refs[4:8], refs[8], refs[9], refs[10]
    step = sources[0].shape[0] // PIECES
    pairs = []
    for a in range(4):
        for i in range(PIECES):
            rows = pl.ds(i * step, step)
            mid = held.at[a, rows]
            pairs.append(
                (
                    pltpu.make_async_copy(sources[a].at[rows], mid, arrive.at[a, i]),
                    pltpu.make_async_copy(mid, targets[a].at[rows], leave.at[a, i]),
                )
            )
    for load, _ in pairs:
        load.start()
    for load, store in pairs:
        load.wait()
        store.start()
    for _, store in pairs:
        store.wait()


def on_device(queries, keys, values, grad_out, summary_lists):
    rows, width = queries.shape
    groups = lax.axis_size("ctx") // GRP
    every = groups * GRP * 2 // SUMS // GRP
    slots = 2 * groups - 1

    bf16, f32 = jnp.bfloat16, jnp.float32
    dma = pltpu.SemaphoreType.DMA
    anywhere = pl.BlockSpec(memory_space=pl.ANY)
    shapes = [jax.ShapeDtypeStruct((rows, width), bf16)] * 4
    results = pl.pallas_call(
        functools.partial(kernel, groups, every),
        out_shape=shapes,
        in_specs=[anywhere] * 4 + [pl.BlockSpec(memory_space=pltpu.SMEM)],
        out_specs=[anywhere] * 4,
        scratch_shapes=[
            pltpu.VMEM((GRP, HG, 2, 2, BLK, HS), bf16),
            pltpu.VMEM((GRP, HG, 2, rows, HS), bf16),
            pltpu.VMEM((slots, HG, 2, BLK, HS), bf16),
        ]
        + [pltpu.VMEM((GRP, HG, rows, HS), bf16)] * 4
        + [
            pltpu.VMEM((slots, 2, BLK, HS), f32),
            pltpu.VMEM((slots, HG, 2, BLK, HS), bf16),
            pltpu.VMEM((2, groups, HG, 2, BLK, HS), bf16),
            pltpu.VMEM((2, HG, 2, BLK, HS), f32),
            pltpu.VMEM((2, HG, 2, BLK, HS), bf16),
            pltpu.VMEM((2, slots, 1, GRP * BLK), f32),
            dma((4,)),
            dma((HG, GRP)),
            dma((HG, GRP)),
            dma((HG, GRP)),
            dma((HG,)),
            dma((HG,)),
            dma((2, groups, HG)),
            dma((slots, HG)),
            dma((slots, HG)),
            dma((2, groups, HG)),
            dma((4,)),
            dma((4,)),
            dma((4,)),
        ],
        compiler_params=pltpu.CompilerParams(
            collective_id=0, has_side_effects=True, vmem_limit_bytes=56 * 1024 * 1024
        ),
        cost_estimate=pl.CostEstimate(
            flops=6 * 10**9, bytes_accessed=8 * 10**6, transcendentals=3 * 10**6
        ),
    )(queries, keys, values, grad_out, summary_lists)
    return pl.pallas_call(
        place,
        out_shape=shapes,
        in_specs=[anywhere] * 4,
        out_specs=[anywhere] * 4,
        scratch_shapes=[pltpu.VMEM((4, rows, width), bf16), dma((4, PIECES)), dma((4, PIECES))],
        compiler_params=pltpu.CompilerParams(vmem_limit_bytes=60 * 1024 * 1024),
        cost_estimate=pl.CostEstimate(flops=0, bytes_accessed=6 * 10**6, transcendentals=0),
    )(*results)


def solution(mesh):
    rows = P(("dp", "ctx"), None)
    return jax.shard_map(
        on_device,
        mesh=mesh,
        in_specs=(rows, rows, rows, rows, P("dp", None)),
        out_specs=(rows, rows, rows, rows),
        check_vma=False,
    )
```

```python
import functools

import jax
import jax.numpy as jnp
from jax import lax
from jax.experimental import pallas as pl
from jax.experimental.pallas import tpu as pltpu
from jax.sharding import PartitionSpec as P

H = 12
HS = 128
BLK = 128
SUMS = 8
PICKS = 4
GRP = 4
HG = H // GRP
WID = HG * HS
HIDDEN = -1e30
LOG2_E = 1.4426950408889634
MESH = pl.DeviceIdType.MESH


def both(*terms):
    return functools.reduce(jnp.logical_and, terms)


def either(*terms):
    return functools.reduce(jnp.logical_or, terms)


def home(span, groups):
    return jnp.where(span < groups, span, 2 * groups - 1 - span)


def is_summary(span, every):
    return lax.rem(jnp.asarray(span + 1, jnp.int32), jnp.int32(every)) == 0


def needed(span, group, groups, every):
    span = jnp.asarray(span, jnp.int32)
    group = jnp.asarray(group, jnp.int32)
    return both(
        span <= 2 * groups - 2 - group,
        home(span, groups) != group,
        either(is_summary(span, every), span + 1 == group, span + 1 == 2 * groups - 1 - group),
    )


def dot_nn(a, b):
    return lax.dot_general(a, b, (((1,), (0,)), ((), ())), preferred_element_type=jnp.float32)


def member_rows(half, k):
    return (k, slice(0, BLK)) if half == 0 else (GRP - 1 - k, slice(BLK, 2 * BLK))


def kernel(
    groups,
    every,
    q_in, k_in, v_in, g_in, lists,
    o_out, dq_out, dk_out, dv_out,
    kv_all, qg_all, kv_buf, qg_buf, kvs,
    o_buf, dq_buf, dk_buf, dv_buf,
    sacc, gstage, grecv, last_acc, late,
    bias, load, in_send, first_recv, rest_recv, qg_recv, loc_kv, loc_qg,
    z_send, z_recv, g_send, g_recv, out_send, out_recv, loc_out,
):
    spans = 2 * groups
    slots = spans - 1
    here = lax.axis_index("ctx")
    group = here // GRP
    member = lax.rem(here, GRP)
    scale = HS ** (-0.5)
    scale_2 = scale * LOG2_E

    barrier = pltpu.get_barrier_semaphore()
    for off in range(1, GRP):
        peer = group * GRP + lax.rem(member + off, GRP)
        pl.semaphore_signal(barrier, inc=1, device_id={"ctx": peer}, device_id_type=MESH)
    for off in range(1, groups):
        peer = lax.rem(group + off, groups) * GRP + member
        pl.semaphore_signal(barrier, inc=1, device_id={"ctx": peer}, device_id_type=MESH)

    def head_cols(m, h):
        return pl.ds(pl.multiple_of((m * HG + h) * HS, HS), HS)

    for i in range(H):
        cols = pl.ds(i * HS, HS)
        for half in range(2):
            rows = pl.ds(half * BLK, BLK)
            for kv, ref in enumerate((k_in, v_in)):
                pltpu.make_async_copy(
                    ref.at[rows, cols], kv_all.at[i, half, kv], load.at[0]
                ).start()
        for j, ref in enumerate((q_in, g_in)):
            pltpu.make_async_copy(ref.at[:, cols], qg_all.at[i, j], load.at[1]).start()
    for h in range(HG):
        cols = head_cols(member, h)
        for half in range(2):
            rows = pl.ds(half * BLK, BLK)
            for kv, ref in enumerate((k_in, v_in)):
                pltpu.make_async_copy(
                    ref.at[rows, cols], kv_buf.at[member, h, half, kv], loc_kv.at[h]
                ).start()
        for i, ref in enumerate((q_in, g_in)):
            pltpu.make_async_copy(ref.at[:, cols], qg_buf.at[member, h, i], loc_qg.at[h]).start()
    for s in range(slots):

        @pl.when(both(jnp.logical_not(needed(s, group, groups, every)), group != s))
        def _():
            kvs[s] = jnp.zeros(kvs.shape[1:], kvs.dtype)

    pl.semaphore_wait(barrier, GRP - 1 + groups - 1)

    front = jnp.where(member < 2, 1, 0)

    def send_kv(h, half, recv):
        for m in range(GRP):

            @pl.when(member != m)
            def _():
                pltpu.make_async_remote_copy(
                    src_ref=kv_all.at[m * HG + h, half],
                    dst_ref=kv_buf.at[member, h, half],
                    send_sem=in_send.at[0],
                    recv_sem=recv.at[h, member],
                    device_id={"ctx": group * GRP + m},
                    device_id_type=MESH,
                ).start()

    def send_qg(h):
        for m in range(GRP):

            @pl.when(member != m)
            def _():
                pltpu.make_async_remote_copy(
                    src_ref=qg_all.at[m * HG + h],
                    dst_ref=qg_buf.at[member, h],
                    send_sem=in_send.at[1],
                    recv_sem=qg_recv.at[h, member],
                    device_id={"ctx": group * GRP + m},
                    device_id_type=MESH,
                ).start()

    pltpu.make_async_copy(kv_all, kv_all, load.at[0]).wait()
    pltpu.make_async_copy(qg_all, qg_all, load.at[1]).wait()
    send_kv(0, front, first_recv)
    send_kv(0, 1 - front, rest_recv)
    send_qg(0)
    send_kv(1, front, first_recv)

    def span_copy(which, p, h):
        span = group if which == 0 else spans - 1 - group
        m = GRP - 1 if which == 0 else 0
        slot = jnp.minimum(span, slots - 1)
        return needed(span, p, groups, every), pltpu.make_async_remote_copy(
            src_ref=kv_buf.at[m, h, which],
            dst_ref=kvs.at[slot, h],
            send_sem=z_send.at[which, p, h],
            recv_sem=z_recv.at[slot, h],
            device_id={"ctx": p * GRP + member},
            device_id_type=MESH,
        )

    def spread(h):
        mine = kv_buf.at[member, h]
        pltpu.make_async_copy(mine, mine, loc_kv.at[h]).wait()
        for m in range(GRP):

            @pl.when(member != m)
            def _():
                ref = kv_buf.at[m, h, 1 if m < 2 else 0]
                pltpu.make_async_copy(ref, ref, first_recv.at[h, m]).wait()

        for p in range(groups):
            for which in range(2):
                wanted, copy = span_copy(which, p, h)

                @pl.when(wanted)
                def _():
                    copy.start()

        kvs[group, h] = kv_buf[GRP - 1, h, 0]

    def gather(h):
        mine = qg_buf.at[member, h]
        pltpu.make_async_copy(mine, mine, loc_qg.at[h]).wait()
        for m in range(GRP):

            @pl.when(member != m)
            def _():
                ref = kv_buf.at[m, h, 0 if m < 2 else 1]
                pltpu.make_async_copy(ref, ref, rest_recv.at[h, m]).wait()
                ref = qg_buf.at[m, h]
                pltpu.make_async_copy(ref, ref, qg_recv.at[h, m]).wait()

        for s in range(slots):

            @pl.when(needed(s, group, groups, every))
            def _():
                pltpu.make_async_copy(kvs.at[s, h], kvs.at[s, h], z_recv.at[s, h]).wait()

    for half in range(2):
        for k in range(GRP):
            block = (group if half == 0 else spans - 1 - group) * GRP + k
            picks = [lists[i, block] for i in range(PICKS)]
            for s in range(slots):
                end = s * GRP + GRP - 1
                seen = end == block - 1
                if (s + 1) % every == 0:
                    picked = either(*[pick == (s + 1) // every - 1 for pick in picks])
                    seen = either(seen, both(picked, end < block - 1))
                row = jnp.full((1, BLK), jnp.where(seen, 0.0, HIDDEN), jnp.float32)
                bias[half, s, :, k * BLK : (k + 1) * BLK] = row

    spread(0)
    send_kv(1, 1 - front, rest_recv)

    key_at = lax.broadcasted_iota(jnp.int32, (BLK, BLK), 0)
    query_at = lax.broadcasted_iota(jnp.int32, (BLK, BLK), 1)
    own_bias = jnp.where(key_at <= query_at, 0.0, HIDDEN).astype(jnp.float32)

    def one_span(half, n, h, k_sum, v_sum, k_sum_t, v_sum_t):
        at = [member_rows(half, k) for k in range(GRP)]
        q = [qg_buf[m, h, 0, r, :] for m, r in at]
        g = [qg_buf[m, h, 1, r, :] for m, r in at]
        kb = [kv_buf[m, h, half, 0] for m, r in at]
        vb = [kv_buf[m, h, half, 1] for m, r in at]
        q_all = jnp.concatenate(q, axis=0)
        g_all = jnp.concatenate(g, axis=0)
        q_t = jnp.transpose(q_all)
        g_t = jnp.transpose(g_all)
        k_two = [jnp.concatenate([kb[max(k - 1, 0)], kb[k]], axis=0) for k in range(GRP)]
        v_two = [jnp.concatenate([vb[max(k - 1, 0)], vb[k]], axis=0) for k in range(GRP)]
        kb_t = [jnp.transpose(block) for block in kb]
        vb_t = [jnp.transpose(block) for block in vb]
        k_two_t = [jnp.concatenate([kb_t[max(k - 1, 0)], kb_t[k]], axis=1) for k in range(GRP)]
        v_two_t = [jnp.concatenate([vb_t[max(k - 1, 0)], vb_t[k]], axis=1) for k in range(GRP)]
        lanes = [slice(k * BLK, (k + 1) * BLK) for k in range(GRP)]

        s_sum = dot_nn(k_sum, q_t).reshape(n, BLK, GRP * BLK)
        local = []
        for k in range(GRP):
            before = jnp.full((BLK, BLK), HIDDEN if k == 0 else 0.0, jnp.float32)
            mask = jnp.concatenate([before, own_bias], axis=0)
            local.append(dot_nn(k_two[k], q_t[:, lanes[k]]) * scale_2 + mask)
        s_loc = jnp.concatenate(local, axis=1)
        hide = bias[half, 0:n]
        top_sum = jnp.max(s_sum, axis=1, keepdims=True) * scale_2 + hide
        top = jnp.maximum(jnp.max(top_sum, axis=0), jnp.max(s_loc, axis=0, keepdims=True))
        p_sum = jnp.exp2(s_sum * scale_2 + (hide - top[None])).reshape(n * BLK, GRP * BLK)
        p_loc = jnp.exp2(s_loc - top)
        total = jnp.sum(p_sum, axis=0, keepdims=True) + jnp.sum(p_loc, axis=0, keepdims=True)
        inv = 1.0 / total
        p_sum = p_sum * inv
        p_loc = p_loc * inv
        low_sum = p_sum.astype(jnp.bfloat16)
        low_loc = p_loc.astype(jnp.bfloat16)

        o_t = dot_nn(v_sum_t, low_sum) + jnp.concatenate(
            [dot_nn(v_two_t[k], low_loc[:, lanes[k]]) for k in range(GRP)], axis=1
        )
        o_t = o_t.astype(jnp.bfloat16)
        delta = jnp.sum(
            g_t.astype(jnp.float32) * o_t.astype(jnp.float32), axis=0, keepdims=True
        )
        attended = jnp.transpose(o_t)

        dp_sum = dot_nn(v_sum, g_t)
        dp_loc = jnp.concatenate([dot_nn(v_two[k], g_t[:, lanes[k]]) for k in range(GRP)], axis=1)
        ds_sum = (p_sum * (dp_sum - delta)).astype(jnp.bfloat16)
        ds_loc = (p_loc * (dp_loc - delta)).astype(jnp.bfloat16)
        dq_t = dot_nn(k_sum_t, ds_sum) + jnp.concatenate(
            [dot_nn(k_two_t[k], ds_loc[:, lanes[k]]) for k in range(GRP)], axis=1
        )
        grad_q = jnp.transpose((dq_t * scale).astype(jnp.bfloat16))
        for k, (m, r) in enumerate(at):
            o_buf[m, h, r, :] = attended[lanes[k], :]
            dq_buf[m, h, r, :] = grad_q[lanes[k], :]

        dk_sum = (dot_nn(ds_sum, q_all) * scale).reshape(n, BLK, HS)
        dv_sum = dot_nn(low_sum, g_all).reshape(n, BLK, HS)
        dk_two = [dot_nn(ds_loc[:, lanes[k]], q[k]) * scale for k in range(GRP)]
        dv_two = [dot_nn(low_loc[:, lanes[k]], g[k]) for k in range(GRP)]
        for two, buf, kv in ((dk_two, dk_buf, 0), (dv_two, dv_buf, 1)):
            for k, (m, r) in enumerate(at):
                if k < GRP - 1:
                    buf[m, h, r, :] = (two[k][BLK:] + two[k + 1][:BLK]).astype(jnp.bfloat16)
                else:
                    last_acc[half, h, kv] = two[k][BLK:]
        return dk_sum, dv_sum

    outs = (o_out, dq_out, dk_out, dv_out)
    obufs = (o_buf, dq_buf, dk_buf, dv_buf)

    def grad_copy(s, h):
        return pltpu.make_async_remote_copy(
            src_ref=gstage.at[s, h],
            dst_ref=grecv.at[0 if s < groups else 1, group, h],
            send_sem=g_send.at[s, h],
            recv_sem=g_recv.at[0 if s < groups else 1, group, h],
            device_id={"ctx": (s if s < groups else spans - 1 - s) * GRP + member},
            device_id_type=MESH,
        )

    def send_out(a, src, rows, m, h):
        place_at = member * HG + h

        @pl.when(member != m)
        def _():
            pltpu.make_async_remote_copy(
                src_ref=src,
                dst_ref=outs[a].at[place_at, rows, :],
                send_sem=out_send.at[a],
                recv_sem=out_recv.at[a],
                device_id={"ctx": group * GRP + m},
                device_id_type=MESH,
            ).start()

        @pl.when(member == m)
        def _():
            pltpu.make_async_copy(src, outs[a].at[place_at, rows, :], loc_out.at[a]).start()

    def finish_head(h):
        for which in range(2):
            span = group if which == 0 else spans - 1 - group
            for p in range(groups):

                @pl.when(needed(span, p, groups, every))
                def _():
                    ref = grecv.at[which, p, h]
                    pltpu.make_async_copy(ref, ref, g_recv.at[which, p, h]).wait()
                    last_acc[which, h] += grecv[which, p, h].astype(jnp.float32)

            late[which, h] = last_acc[which, h].astype(jnp.bfloat16)
            m = GRP - 1 if which == 0 else 0
            rows = pl.ds(which * BLK, BLK)
            for kv in range(2):
                send_out(2 + kv, late.at[which, h, kv], rows, m, h)

    def one_head(h, carry):
        n_low = groups - 1
        gather(h)

        @pl.when(h + 1 < HG)
        def _():
            send_qg(h + 1)

            @pl.when(h + 2 < HG)
            def _():
                send_kv(h + 2, front, first_recv)

            spread(h + 1)

        k_sum = kvs[0:slots, h, 0].reshape(slots * BLK, HS)
        v_sum = kvs[0:slots, h, 1].reshape(slots * BLK, HS)
        k_sum_t = jnp.transpose(k_sum)
        v_sum_t = jnp.transpose(v_sum)

        def ship(first, end):
            for s in range(first, end):

                @pl.when(needed(s, group, groups, every))
                def _():
                    gstage[s, h] = sacc[s].astype(jnp.bfloat16)
                    grad_copy(s, h).start()

        dk_sum, dv_sum = one_span(1, slots, h, k_sum, v_sum, k_sum_t, v_sum_t)
        sacc[:, 0] = dk_sum
        sacc[:, 1] = dv_sum
        ship(n_low, slots)
        low = n_low * BLK
        dk_sum, dv_sum = one_span(
            0, n_low, h, k_sum[:low], v_sum[:low], k_sum_t[:, :low], v_sum_t[:, :low]
        )
        sacc[0:n_low, 0] += dk_sum
        sacc[0:n_low, 1] += dv_sum
        ship(0, n_low)
        last_acc[0, h] += sacc[group]
        for a in range(4):
            for m in range(GRP):
                if a < 2 or m in (1, 2):
                    rows = pl.ds(0, 2 * BLK)
                else:
                    rows = pl.ds(0 if m == 0 else BLK, BLK)
                send_out(a, obufs[a].at[m, h, rows, :], rows, m, h)

        @pl.when(h + 2 < HG)
        def _():
            send_kv(h + 2, 1 - front, rest_recv)

        @pl.when(h > 0)
        def _():
            finish_head(h - 1)

        return carry

    lax.fori_loop(0, HG, one_head, 0)

    finish_head(HG - 1)

    for i, ref in enumerate((kv_all, qg_all)):
        away = ref.at[pl.ds(0, (GRP - 1) * HG)]
        pltpu.make_async_copy(away, away, in_send.at[i]).wait()
    for p in range(groups):
        for which in range(2):
            for h in range(HG):
                wanted, copy = span_copy(which, p, h)

                @pl.when(wanted)
                def _():
                    copy.wait_send()

    for s in range(slots):

        @pl.when(needed(s, group, groups, every))
        def _():
            for h in range(HG):
                grad_copy(s, h).wait_send()

    for a in range(4):
        own = outs[a].at[pl.ds(0, HG)]
        away = outs[a].at[pl.ds(0, (GRP - 1) * HG)]
        pltpu.make_async_copy(own, own, loc_out.at[a]).wait()
        pltpu.make_async_copy(away, away, out_send.at[a]).wait()
        pltpu.make_async_copy(away, away, out_recv.at[a]).wait()


def place(*refs):
    sources, targets, held, arrive, leave = refs[:4], refs[4:8], refs[8], refs[9], refs[10]
    for a in range(4):
        for i in range(H):
            pltpu.make_async_copy(
                sources[a].at[i], held.at[a, :, pl.ds(i * HS, HS)], arrive.at[a]
            ).start()
    for a in range(4):
        pltpu.make_async_copy(held.at[a], held.at[a], arrive.at[a]).wait()
        pltpu.make_async_copy(held.at[a], targets[a], leave.at[a]).start()
    for a in range(4):
        pltpu.make_async_copy(held.at[a], targets[a], leave.at[a]).wait()


def on_device(queries, keys, values, grad_out, summary_lists):
    rows, width = queries.shape
    groups = lax.axis_size("ctx") // GRP
    every = groups * GRP * 2 // SUMS // GRP
    slots = 2 * groups - 1

    bf16, f32 = jnp.bfloat16, jnp.float32
    dma = pltpu.SemaphoreType.DMA
    anywhere = pl.BlockSpec(memory_space=pl.ANY)
    shapes = [jax.ShapeDtypeStruct((rows, width), bf16)] * 4
    results = pl.pallas_call(
        functools.partial(kernel, groups, every),
        out_shape=[jax.ShapeDtypeStruct((H, rows, HS), bf16)] * 4,
        in_specs=[anywhere] * 4 + [pl.BlockSpec(memory_space=pltpu.SMEM)],
        out_specs=[anywhere] * 4,
        scratch_shapes=[
            pltpu.VMEM((H, 2, 2, BLK, HS), bf16),
            pltpu.VMEM((H, 2, rows, HS), bf16),
            pltpu.VMEM((GRP, HG, 2, 2, BLK, HS), bf16),
            pltpu.VMEM((GRP, HG, 2, rows, HS), bf16),
            pltpu.VMEM((slots, HG, 2, BLK, HS), bf16),
        ]
        + [pltpu.VMEM((GRP, HG, rows, HS), bf16)] * 4
        + [
            pltpu.VMEM((slots, 2, BLK, HS), f32),
            pltpu.VMEM((slots, HG, 2, BLK, HS), bf16),
            pltpu.VMEM((2, groups, HG, 2, BLK, HS), bf16),
            pltpu.VMEM((2, HG, 2, BLK, HS), f32),
            pltpu.VMEM((2, HG, 2, BLK, HS), bf16),
            pltpu.VMEM((2, slots, 1, GRP * BLK), f32),
            dma((2,)),
            dma((2,)),
            dma((HG, GRP)),
            dma((HG, GRP)),
            dma((HG, GRP)),
            dma((HG,)),
            dma((HG,)),
            dma((2, groups, HG)),
            dma((slots, HG)),
            dma((slots, HG)),
            dma((2, groups, HG)),
            dma((4,)),
            dma((4,)),
            dma((4,)),
        ],
        compiler_params=pltpu.CompilerParams(
            collective_id=0, has_side_effects=True, vmem_limit_bytes=56 * 1024 * 1024
        ),
        cost_estimate=pl.CostEstimate(
            flops=6 * 10**9, bytes_accessed=8 * 10**6, transcendentals=3 * 10**6
        ),
    )(queries, keys, values, grad_out, summary_lists.T)
    return pl.pallas_call(
        place,
        out_shape=shapes,
        in_specs=[anywhere] * 4,
        out_specs=[anywhere] * 4,
        scratch_shapes=[pltpu.VMEM((4, rows, width), bf16), dma((4,)), dma((4,))],
        compiler_params=pltpu.CompilerParams(vmem_limit_bytes=60 * 1024 * 1024),
        cost_estimate=pl.CostEstimate(flops=0, bytes_accessed=6 * 10**6, transcendentals=0),
    )(*results)


def solution(mesh):
    rows = P(("dp", "ctx"), None)
    return jax.shard_map(
        on_device,
        mesh=mesh,
        in_specs=(rows, rows, rows, rows, P("dp", None)),
        out_specs=(rows, rows, rows, rows),
        check_vma=False,
    )
```

```python
import functools

import jax
import jax.numpy as jnp
from jax import lax
from jax.experimental import pallas as pl
from jax.experimental.pallas import tpu as pltpu
from jax.sharding import PartitionSpec as P

H = 12
HS = 128
BLK = 128
SUMS = 8
PICKS = 4
GRP = 4
HG = H // GRP
WID = HG * HS
HIDDEN = -1e30
LOG2_E = 1.4426950408889634
MESH = pl.DeviceIdType.MESH


def both(*terms):
    return functools.reduce(jnp.logical_and, terms)


def either(*terms):
    return functools.reduce(jnp.logical_or, terms)


def home(span, groups):
    return jnp.where(span < groups, span, 2 * groups - 1 - span)


def is_summary(span, every):
    return lax.rem(jnp.asarray(span + 1, jnp.int32), jnp.int32(every)) == 0


def needed(span, group, groups, every):
    span = jnp.asarray(span, jnp.int32)
    group = jnp.asarray(group, jnp.int32)
    return both(
        span <= 2 * groups - 2 - group,
        home(span, groups) != group,
        either(is_summary(span, every), span + 1 == group, span + 1 == 2 * groups - 1 - group),
    )


def dot_nn(a, b):
    return lax.dot_general(a, b, (((1,), (0,)), ((), ())), preferred_element_type=jnp.float32)


def member_rows(half, k):
    return (k, slice(0, BLK)) if half == 0 else (GRP - 1 - k, slice(BLK, 2 * BLK))


def kernel(
    groups,
    every,
    q_in, k_in, v_in, g_in, lists,
    o_out, dq_out, dk_out, dv_out,
    kv_all, qg_all, kv_buf, qg_buf, kvs,
    o_buf, dq_buf, dk_buf, dv_buf,
    sacc, gstage, grecv, last_acc, late,
    bias, load, in_send, first_recv, rest_recv, qg_recv, loc_kv, loc_qg,
    z_send, z_recv, g_send, g_recv, out_send, out_recv, loc_out,
):
    spans = 2 * groups
    slots = spans - 1
    here = lax.axis_index("ctx")
    group = here // GRP
    member = lax.rem(here, GRP)
    scale = HS ** (-0.5)
    scale_2 = scale * LOG2_E

    barrier = pltpu.get_barrier_semaphore()
    for off in range(1, GRP):
        peer = group * GRP + lax.rem(member + off, GRP)
        pl.semaphore_signal(barrier, inc=1, device_id={"ctx": peer}, device_id_type=MESH)
    for off in range(1, groups):
        peer = lax.rem(group + off, groups) * GRP + member
        pl.semaphore_signal(barrier, inc=1, device_id={"ctx": peer}, device_id_type=MESH)

    def head_cols(m, h):
        return pl.ds(pl.multiple_of((m * HG + h) * HS, HS), HS)

    for i in range(H):
        for j, ref in enumerate((k_in, v_in)):
            pltpu.make_async_copy(ref.at[:, pl.ds(i * HS, HS)], kv_all.at[i, j], load.at[0]).start()
    for i in range(H):
        for j, ref in enumerate((q_in, g_in)):
            pltpu.make_async_copy(ref.at[:, pl.ds(i * HS, HS)], qg_all.at[i, j], load.at[1]).start()
    for h in range(HG):
        cols = head_cols(member, h)
        for half in range(2):
            rows = pl.ds(half * BLK, BLK)
            for kv, ref in enumerate((k_in, v_in)):
                pltpu.make_async_copy(
                    ref.at[rows, cols], kv_buf.at[member, h, half, kv], loc_kv.at[h]
                ).start()
        for i, ref in enumerate((q_in, g_in)):
            pltpu.make_async_copy(ref.at[:, cols], qg_buf.at[member, h, i], loc_qg.at[h]).start()
    for s in range(slots):

        @pl.when(both(jnp.logical_not(needed(s, group, groups, every)), group != s))
        def _():
            kvs[s] = jnp.zeros(kvs.shape[1:], kvs.dtype)

    pl.semaphore_wait(barrier, GRP - 1 + groups - 1)

    front = jnp.where(member < 2, 1, 0)

    def send_kv(h, half, recv):
        rows = pl.ds(pl.multiple_of(half * BLK, BLK), BLK)
        for m in range(GRP):

            @pl.when(member != m)
            def _():
                pltpu.make_async_remote_copy(
                    src_ref=kv_all.at[m * HG + h, :, rows, :],
                    dst_ref=kv_buf.at[member, h, half],
                    send_sem=in_send.at[0],
                    recv_sem=recv.at[h, member],
                    device_id={"ctx": group * GRP + m},
                    device_id_type=MESH,
                ).start()

    def send_qg(h):
        for m in range(GRP):

            @pl.when(member != m)
            def _():
                pltpu.make_async_remote_copy(
                    src_ref=qg_all.at[m * HG + h],
                    dst_ref=qg_buf.at[member, h],
                    send_sem=in_send.at[1],
                    recv_sem=qg_recv.at[h, member],
                    device_id={"ctx": group * GRP + m},
                    device_id_type=MESH,
                ).start()

    pltpu.make_async_copy(kv_all, kv_all, load.at[0]).wait()
    send_kv(0, front, first_recv)
    send_kv(0, 1 - front, rest_recv)
    pltpu.make_async_copy(qg_all, qg_all, load.at[1]).wait()
    send_qg(0)
    send_kv(1, front, first_recv)

    def span_copy(which, p, h):
        span = group if which == 0 else spans - 1 - group
        m = GRP - 1 if which == 0 else 0
        slot = jnp.minimum(span, slots - 1)
        return needed(span, p, groups, every), pltpu.make_async_remote_copy(
            src_ref=kv_buf.at[m, h, which],
            dst_ref=kvs.at[slot, h],
            send_sem=z_send.at[which, p, h],
            recv_sem=z_recv.at[slot, h],
            device_id={"ctx": p * GRP + member},
            device_id_type=MESH,
        )

    def spread(h):
        mine = kv_buf.at[member, h]
        pltpu.make_async_copy(mine, mine, loc_kv.at[h]).wait()
        for m in range(GRP):

            @pl.when(member != m)
            def _():
                ref = kv_buf.at[m, h, 1 if m < 2 else 0]
                pltpu.make_async_copy(ref, ref, first_recv.at[h, m]).wait()

        for p in range(groups):
            for which in range(2):
                wanted, copy = span_copy(which, p, h)

                @pl.when(wanted)
                def _():
                    copy.start()

        kvs[group, h] = kv_buf[GRP - 1, h, 0]

    def gather(h):
        mine = qg_buf.at[member, h]
        pltpu.make_async_copy(mine, mine, loc_qg.at[h]).wait()
        for m in range(GRP):

            @pl.when(member != m)
            def _():
                ref = kv_buf.at[m, h, 0 if m < 2 else 1]
                pltpu.make_async_copy(ref, ref, rest_recv.at[h, m]).wait()
                ref = qg_buf.at[m, h]
                pltpu.make_async_copy(ref, ref, qg_recv.at[h, m]).wait()

        for s in range(slots):

            @pl.when(needed(s, group, groups, every))
            def _():
                pltpu.make_async_copy(kvs.at[s, h], kvs.at[s, h], z_recv.at[s, h]).wait()

    for half in range(2):
        for k in range(GRP):
            block = (group if half == 0 else spans - 1 - group) * GRP + k
            picks = [lists[i, block] for i in range(PICKS)]
            for s in range(slots):
                end = s * GRP + GRP - 1
                seen = end == block - 1
                if (s + 1) % every == 0:
                    picked = either(*[pick == (s + 1) // every - 1 for pick in picks])
                    seen = either(seen, both(picked, end < block - 1))
                row = jnp.full((1, BLK), jnp.where(seen, 0.0, HIDDEN), jnp.float32)
                bias[half, s, :, k * BLK : (k + 1) * BLK] = row

    spread(0)
    send_kv(1, 1 - front, rest_recv)

    key_at = lax.broadcasted_iota(jnp.int32, (BLK, BLK), 0)
    query_at = lax.broadcasted_iota(jnp.int32, (BLK, BLK), 1)
    own_bias = jnp.where(key_at <= query_at, 0.0, HIDDEN).astype(jnp.float32)

    def one_span(half, n, h, k_sum, v_sum, k_sum_t, v_sum_t):
        at = [member_rows(half, k) for k in range(GRP)]
        q = [qg_buf[m, h, 0, r, :] for m, r in at]
        g = [qg_buf[m, h, 1, r, :] for m, r in at]
        kb = [kv_buf[m, h, half, 0] for m, r in at]
        vb = [kv_buf[m, h, half, 1] for m, r in at]
        q_all = jnp.concatenate(q, axis=0)
        g_all = jnp.concatenate(g, axis=0)
        q_t = jnp.transpose(q_all)
        g_t = jnp.transpose(g_all)
        k_two = [jnp.concatenate([kb[max(k - 1, 0)], kb[k]], axis=0) for k in range(GRP)]
        v_two = [jnp.concatenate([vb[max(k - 1, 0)], vb[k]], axis=0) for k in range(GRP)]
        kb_t = [jnp.transpose(block) for block in kb]
        vb_t = [jnp.transpose(block) for block in vb]
        k_two_t = [jnp.concatenate([kb_t[max(k - 1, 0)], kb_t[k]], axis=1) for k in range(GRP)]
        v_two_t = [jnp.concatenate([vb_t[max(k - 1, 0)], vb_t[k]], axis=1) for k in range(GRP)]
        lanes = [slice(k * BLK, (k + 1) * BLK) for k in range(GRP)]

        s_sum = dot_nn(k_sum, q_t).reshape(n, BLK, GRP * BLK)
        local = []
        for k in range(GRP):
            before = jnp.full((BLK, BLK), HIDDEN if k == 0 else 0.0, jnp.float32)
            mask = jnp.concatenate([before, own_bias], axis=0)
            local.append(dot_nn(k_two[k], q_t[:, lanes[k]]) * scale_2 + mask)
        s_loc = jnp.concatenate(local, axis=1)
        hide = bias[half, 0:n]
        top_sum = jnp.max(s_sum, axis=1, keepdims=True) * scale_2 + hide
        top = jnp.maximum(jnp.max(top_sum, axis=0), jnp.max(s_loc, axis=0, keepdims=True))
        p_sum = jnp.exp2(s_sum * scale_2 + (hide - top[None])).reshape(n * BLK, GRP * BLK)
        p_loc = jnp.exp2(s_loc - top)
        total = jnp.sum(p_sum, axis=0, keepdims=True) + jnp.sum(p_loc, axis=0, keepdims=True)
        inv = 1.0 / total
        p_sum = p_sum * inv
        p_loc = p_loc * inv
        low_sum = p_sum.astype(jnp.bfloat16)
        low_loc = p_loc.astype(jnp.bfloat16)

        o_t = dot_nn(v_sum_t, low_sum) + jnp.concatenate(
            [dot_nn(v_two_t[k], low_loc[:, lanes[k]]) for k in range(GRP)], axis=1
        )
        o_t = o_t.astype(jnp.bfloat16)
        delta = jnp.sum(
            g_t.astype(jnp.float32) * o_t.astype(jnp.float32), axis=0, keepdims=True
        )
        attended = jnp.transpose(o_t)

        dp_sum = dot_nn(v_sum, g_t)
        dp_loc = jnp.concatenate([dot_nn(v_two[k], g_t[:, lanes[k]]) for k in range(GRP)], axis=1)
        ds_sum = (p_sum * (dp_sum - delta)).astype(jnp.bfloat16)
        ds_loc = (p_loc * (dp_loc - delta)).astype(jnp.bfloat16)
        dq_t = dot_nn(k_sum_t, ds_sum) + jnp.concatenate(
            [dot_nn(k_two_t[k], ds_loc[:, lanes[k]]) for k in range(GRP)], axis=1
        )
        grad_q = jnp.transpose((dq_t * scale).astype(jnp.bfloat16))
        for k, (m, r) in enumerate(at):
            o_buf[m, h, r, :] = attended[lanes[k], :]
            dq_buf[m, h, r, :] = grad_q[lanes[k], :]

        dk_sum = (dot_nn(ds_sum, q_all) * scale).reshape(n, BLK, HS)
        dv_sum = dot_nn(low_sum, g_all).reshape(n, BLK, HS)
        dk_two = [dot_nn(ds_loc[:, lanes[k]], q[k]) * scale for k in range(GRP)]
        dv_two = [dot_nn(low_loc[:, lanes[k]], g[k]) for k in range(GRP)]
        for two, buf, kv in ((dk_two, dk_buf, 0), (dv_two, dv_buf, 1)):
            for k, (m, r) in enumerate(at):
                if k < GRP - 1:
                    buf[m, h, r, :] = (two[k][BLK:] + two[k + 1][:BLK]).astype(jnp.bfloat16)
                else:
                    last_acc[half, h, kv] = two[k][BLK:]
        return dk_sum, dv_sum

    outs = (o_out, dq_out, dk_out, dv_out)
    obufs = (o_buf, dq_buf, dk_buf, dv_buf)

    def grad_copy(s, h):
        return pltpu.make_async_remote_copy(
            src_ref=gstage.at[s, h],
            dst_ref=grecv.at[0 if s < groups else 1, group, h],
            send_sem=g_send.at[s, h],
            recv_sem=g_recv.at[0 if s < groups else 1, group, h],
            device_id={"ctx": (s if s < groups else spans - 1 - s) * GRP + member},
            device_id_type=MESH,
        )

    def send_out(a, src, rows, m, h):
        place_at = member * HG + h

        @pl.when(member != m)
        def _():
            pltpu.make_async_remote_copy(
                src_ref=src,
                dst_ref=outs[a].at[place_at, rows, :],
                send_sem=out_send.at[a],
                recv_sem=out_recv.at[a],
                device_id={"ctx": group * GRP + m},
                device_id_type=MESH,
            ).start()

        @pl.when(member == m)
        def _():
            pltpu.make_async_copy(src, outs[a].at[place_at, rows, :], loc_out.at[a]).start()

    def finish_head(h):
        for which in range(2):
            span = group if which == 0 else spans - 1 - group
            for p in range(groups):

                @pl.when(needed(span, p, groups, every))
                def _():
                    ref = grecv.at[which, p, h]
                    pltpu.make_async_copy(ref, ref, g_recv.at[which, p, h]).wait()
                    last_acc[which, h] += grecv[which, p, h].astype(jnp.float32)

            late[which, h] = last_acc[which, h].astype(jnp.bfloat16)
            m = GRP - 1 if which == 0 else 0
            rows = pl.ds(which * BLK, BLK)
            for kv in range(2):
                send_out(2 + kv, late.at[which, h, kv], rows, m, h)

    def one_head(h, carry):
        n_low = groups - 1
        gather(h)

        @pl.when(h + 1 < HG)
        def _():
            send_qg(h + 1)

            @pl.when(h + 2 < HG)
            def _():
                send_kv(h + 2, front, first_recv)

            spread(h + 1)

        k_sum = kvs[0:slots, h, 0].reshape(slots * BLK, HS)
        v_sum = kvs[0:slots, h, 1].reshape(slots * BLK, HS)
        k_sum_t = jnp.transpose(k_sum)
        v_sum_t = jnp.transpose(v_sum)

        def ship(first, end):
            for s in range(first, end):

                @pl.when(needed(s, group, groups, every))
                def _():
                    gstage[s, h] = sacc[s].astype(jnp.bfloat16)
                    grad_copy(s, h).start()

        dk_sum, dv_sum = one_span(1, slots, h, k_sum, v_sum, k_sum_t, v_sum_t)
        sacc[:, 0] = dk_sum
        sacc[:, 1] = dv_sum
        ship(n_low, slots)
        low = n_low * BLK
        dk_sum, dv_sum = one_span(
            0, n_low, h, k_sum[:low], v_sum[:low], k_sum_t[:, :low], v_sum_t[:, :low]
        )
        sacc[0:n_low, 0] += dk_sum
        sacc[0:n_low, 1] += dv_sum
        ship(0, n_low)
        last_acc[0, h] += sacc[group]
        for a in range(4):
            for m in range(GRP):
                if a < 2 or m in (1, 2):
                    rows = pl.ds(0, 2 * BLK)
                else:
                    rows = pl.ds(0 if m == 0 else BLK, BLK)
                send_out(a, obufs[a].at[m, h, rows, :], rows, m, h)

        @pl.when(h + 2 < HG)
        def _():
            send_kv(h + 2, 1 - front, rest_recv)

        @pl.when(h > 0)
        def _():
            finish_head(h - 1)

        return carry

    lax.fori_loop(0, HG, one_head, 0)

    finish_head(HG - 1)

    for i, ref in enumerate((kv_all, qg_all)):
        away = ref.at[pl.ds(0, (GRP - 1) * HG)]
        pltpu.make_async_copy(away, away, in_send.at[i]).wait()
    for p in range(groups):
        for which in range(2):
            for h in range(HG):
                wanted, copy = span_copy(which, p, h)

                @pl.when(wanted)
                def _():
                    copy.wait_send()

    for s in range(slots):

        @pl.when(needed(s, group, groups, every))
        def _():
            for h in range(HG):
                grad_copy(s, h).wait_send()

    for a in range(4):
        own = outs[a].at[pl.ds(0, HG)]
        away = outs[a].at[pl.ds(0, (GRP - 1) * HG)]
        pltpu.make_async_copy(own, own, loc_out.at[a]).wait()
        pltpu.make_async_copy(away, away, out_send.at[a]).wait()
        pltpu.make_async_copy(away, away, out_recv.at[a]).wait()


def place(*refs):
    sources, targets, held, arrive, leave = refs[:4], refs[4:8], refs[8], refs[9], refs[10]
    for a in range(4):
        for i in range(H):
            pltpu.make_async_copy(
                sources[a].at[i], held.at[a, :, pl.ds(i * HS, HS)], arrive.at[a]
            ).start()
    for a in range(4):
        pltpu.make_async_copy(held.at[a], held.at[a], arrive.at[a]).wait()
        pltpu.make_async_copy(held.at[a], targets[a], leave.at[a]).start()
    for a in range(4):
        pltpu.make_async_copy(held.at[a], targets[a], leave.at[a]).wait()


def on_device(queries, keys, values, grad_out, summary_lists):
    rows, width = queries.shape
    groups = lax.axis_size("ctx") // GRP
    every = groups * GRP * 2 // SUMS // GRP
    slots = 2 * groups - 1

    bf16, f32 = jnp.bfloat16, jnp.float32
    dma = pltpu.SemaphoreType.DMA
    anywhere = pl.BlockSpec(memory_space=pl.ANY)
    shapes = [jax.ShapeDtypeStruct((rows, width), bf16)] * 4
    results = pl.pallas_call(
        functools.partial(kernel, groups, every),
        out_shape=[jax.ShapeDtypeStruct((H, rows, HS), bf16)] * 4,
        in_specs=[anywhere] * 4 + [pl.BlockSpec(memory_space=pltpu.SMEM)],
        out_specs=[anywhere] * 4,
        scratch_shapes=[
            pltpu.VMEM((H, 2, rows, HS), bf16),
            pltpu.VMEM((H, 2, rows, HS), bf16),
            pltpu.VMEM((GRP, HG, 2, 2, BLK, HS), bf16),
            pltpu.VMEM((GRP, HG, 2, rows, HS), bf16),
            pltpu.VMEM((slots, HG, 2, BLK, HS), bf16),
        ]
        + [pltpu.VMEM((GRP, HG, rows, HS), bf16)] * 4
        + [
            pltpu.VMEM((slots, 2, BLK, HS), f32),
            pltpu.VMEM((slots, HG, 2, BLK, HS), bf16),
            pltpu.VMEM((2, groups, HG, 2, BLK, HS), bf16),
            pltpu.VMEM((2, HG, 2, BLK, HS), f32),
            pltpu.VMEM((2, HG, 2, BLK, HS), bf16),
            pltpu.VMEM((2, slots, 1, GRP * BLK), f32),
            dma((2,)),
            dma((2,)),
            dma((HG, GRP)),
            dma((HG, GRP)),
            dma((HG, GRP)),
            dma((HG,)),
            dma((HG,)),
            dma((2, groups, HG)),
            dma((slots, HG)),
            dma((slots, HG)),
            dma((2, groups, HG)),
            dma((4,)),
            dma((4,)),
            dma((4,)),
        ],
        compiler_params=pltpu.CompilerParams(
            collective_id=0, has_side_effects=True, vmem_limit_bytes=56 * 1024 * 1024
        ),
        cost_estimate=pl.CostEstimate(
            flops=6 * 10**9, bytes_accessed=8 * 10**6, transcendentals=3 * 10**6
        ),
    )(queries, keys, values, grad_out, summary_lists.T)
    return pl.pallas_call(
        place,
        out_shape=shapes,
        in_specs=[anywhere] * 4,
        out_specs=[anywhere] * 4,
        scratch_shapes=[pltpu.VMEM((4, rows, width), bf16), dma((4,)), dma((4,))],
        compiler_params=pltpu.CompilerParams(vmem_limit_bytes=60 * 1024 * 1024),
        cost_estimate=pl.CostEstimate(flops=0, bytes_accessed=6 * 10**6, transcendentals=0),
    )(*results)


def solution(mesh):
    rows = P(("dp", "ctx"), None)
    return jax.shard_map(
        on_device,
        mesh=mesh,
        in_specs=(rows, rows, rows, rows, P("dp", None)),
        out_specs=(rows, rows, rows, rows),
        check_vma=False,
    )
```
